128 devices in a mesh: grp: 8 (over x, core), seq: 16 (over y, z).
Axes of the slice: x: 4, y: 4, z: 4, core: 2. Of those that a mesh axis runs over, the one named last changes fastest.
Arguments:
- queries: bfloat16 [16384, 4096], P(('grp', 'seq')), may hold values from -6 to 6
- key_rows: bfloat16 [16384, 4096], P(('grp', 'seq')), may hold values from -6 to 6
- value_rows: bfloat16 [16384, 4096], P(('grp', 'seq')), may hold values from -6 to 6
- gate_logits: bfloat16 [16384, 4096], P(('grp', 'seq')), may hold values from -6 to 6
- residual_in: bfloat16 [16384, 4096], P(('grp', 'seq')), may hold values from -6 to 6
- decay_rate: float32 [16384, 32], P(('grp', 'seq')), may hold values from 0 to 1, as said below
- attention_gain: float32 [4096], replicated, may hold values from 0.25 to 1.75
- expert_gain: float32 [4096], replicated, may hold values from 0.25 to 1.75
- expert_index: int32 [16384, 2], P(('grp', 'seq')), may hold values from 0 to 15, all different within a row; in each aligned block of 128 rows (0 to 127, 128 to 255, ...) at most 16 rows name the same one
- router_weight: float32 [16384, 2], P(('grp', 'seq')), may hold values from 0.1 to 0.9
- gate_up_weight: bfloat16 [16, 4096, 2, 4608], P('seq', None, None, 'grp'), may hold values from -0.09375 to 0.09375
- down_weight: bfloat16 [16, 4608, 4096], P('seq', 'grp'), may hold values from -0.09375 to 0.09375
Outputs:
- layer_output: bfloat16 [16384, 4096], P(('grp', 'seq'))
The draws below stay inside these ranges and needn't reach their ends.
Inputs may be any that keep to these rules, and one draw needn't show every extreme that they name: `expert_index`: each expert is named by exactly 16 of the 128 rows of one device; a row names 2 different experts. `decay_rate`: nonnegative rates.
All inputs are finite; a program needn't handle non-finite values.
Results may differ from the reference program's by a relative error of at most 0.02.
Values may be sent and summed in bfloat16 or wider, within the bound.
No kernel may reach another device: no remote copies, remote signals or barrier semaphores. Data moves between devices by JAX's collectives and lax.ppermute only.
A program may use at most 576 MiB of HBM per device.

```python
import math
import jax
import jax.numpy as jnp
import numpy as np
from jax import lax

ATTENTION_HEADS = 32
HEAD = 128
FF = 4608
TOP = 2
TOK_DEV = 128
D = 4096
EXPERTS = 16
HBLK = 576
CAP = 16
SEQUENCE_TOKENS = 16384
N_GRP = 8


def draw_decay_rate(key, part):
    key = jax.random.fold_in(key, 7)
    random_key_variety, random_key_gradual, random_key_quick, random_key_block, random_key_wobble, random_key_spike, random_key_extent = jax.random.split(key, 7)
    fast_share = 0.5
    fast_heads = jax.random.uniform(random_key_variety, (ATTENTION_HEADS,)) < fast_share
    slow_base = jnp.exp(jax.random.uniform(random_key_gradual, (ATTENTION_HEADS,), minval=math.log(0.1), maxval=math.log(0.3))) / SEQUENCE_TOKENS
    fast_base = jnp.exp(jax.random.uniform(random_key_quick, (ATTENTION_HEADS,), minval=math.log(1.0 / 50.0), maxval=math.log(1.0 / 30.0)))
    baseline_rate = jnp.where(fast_heads, fast_base, slow_base)
    block_multiplier = jnp.exp(jax.random.uniform(random_key_block, (SEQUENCE_TOKENS // TOK_DEV, ATTENTION_HEADS), minval=math.log(0.5), maxval=math.log(2.0)))
    block_multiplier = jnp.repeat(block_multiplier, TOK_DEV, axis=0)
    random_wobble = jax.random.uniform(random_key_wobble, (SEQUENCE_TOKENS, ATTENTION_HEADS), minval=0.5, maxval=1.5)
    spike_list = jax.random.uniform(random_key_spike, (SEQUENCE_TOKENS, ATTENTION_HEADS)) < 2.0 / SEQUENCE_TOKENS
    spike_size = jax.random.uniform(random_key_extent, (SEQUENCE_TOKENS, ATTENTION_HEADS), minval=0.22, maxval=0.69)
    decay_result = baseline_rate[None, :] * block_multiplier * random_wobble + jnp.where(spike_list, spike_size, 0.0)
    return decay_result.astype(jnp.float32)


def block_scale(rng, dims, cuts, smallest, top_value):
    level, own = 1.0, jax.random.fold_in(rng, 6)
    for dim, shards_of in cuts:
        draws = jnp.exp(jax.random.uniform(jax.random.fold_in(own, dim), (shards_of,), jnp.float32, smallest / len(cuts), top_value / len(cuts)))
        level = level * jnp.repeat(draws, dims[dim] // shards_of).reshape([-1 if axis == dim else 1 for axis in range(len(dims))])
    return level


def routed_block(key, own, number, rows, number_of, top, bound, skew):
    order = jax.random.permutation(key, number_of)
    packed, common = portions_of(number_of, rows * top, bound, skew, True), portions_of(number_of, rows * top, bound, skew, False)
    places = jnp.arange(number_of)

    def named(sizes, turn):
        used = int((sizes > 0).sum())
        fixed = max(1, used // 4)
        passed = fixed + (places - fixed + turn * (used - fixed)) % max(1, number_of - fixed)
        return jnp.zeros((number_of,), jnp.int32).at[order[jnp.where(places < fixed, places, passed)]].set(jnp.asarray(sizes, jnp.int32))

    sizes = jnp.where(number % 4 == 0, named(packed, number // 4), named(common, number - number // 4 - 1))
    mixed = jax.random.permutation(jax.random.fold_in(own, 3), number_of)
    source_of, receiver = mixed[0:number_of // 2 * 2:2], mixed[1:number_of // 2 * 2:2]
    margin = jnp.minimum(sizes[source_of] - 1, bound - sizes[receiver]) // 2
    margin = jnp.where((source_of == order[0]) | (receiver == order[0]) | (sizes[receiver] == 0), 0, jnp.maximum(margin, 0))
    passed = jax.random.randint(jax.random.fold_in(own, 4), (number_of // 2,), 0, 1 << 20) % (margin + 1)
    sizes = sizes.at[source_of].add(-passed).at[receiver].add(passed)
    labels = jnp.searchsorted(jnp.cumsum(sizes), jnp.arange(rows * top), side="right").astype(jnp.int32)
    grid = labels.reshape(top, rows).T
    grid = grid[jax.random.permutation(jax.random.fold_in(own, 1), rows)]
    turn = jax.random.randint(jax.random.fold_in(own, 2), (rows, 1), 0, top)
    return jnp.take_along_axis(grid, (jnp.arange(top)[None, :] + turn) % top, axis=1)


def portions_of(amount, total, limit, slope, full):
    loads = [(1 << 20) // math.isqrt(grade ** slope) + 1 for grade in range(1, amount + 1)]
    largest = limit if full else min(limit, max(-(-total // amount), total * loads[0] // sum(loads)))
    least = 1 if total - largest >= amount - 1 else 0
    counts, spare = [largest] + [least] * (amount - 1), total - largest - least * (amount - 1)
    while spare > 0:
        free = [i for i in range(1, amount) if counts[i] < largest] or [i for i in range(1, amount) if counts[i] < limit]
        whole, left = sum([loads[i] for i in free]), spare
        for i in free:
            extra = min(limit - counts[i], max(1, left * loads[i] // whole), spare)
            counts[i] = counts[i] + extra
            spare = spare - extra
    return np.array(counts)


def gaussian(rng, dims, width, limit, pieces=(), dtype=jnp.bfloat16):
    drawn = jax.random.normal(rng, dims, jnp.float32) * width
    if len(pieces) > 0:
        drawn = block_scale(rng, dims, pieces, -0.22, 0.18) * drawn
    return jnp.clip(drawn, min=-limit, max=limit).astype(dtype)


def setup_inputs(seed: int = 0) -> dict:
    key_list = jax.random.split(jax.random.key(seed), 13)
    queries = gaussian(key_list[0], (SEQUENCE_TOKENS, D), 1.0, 6.0, ((0, 128),))
    key_rows = gaussian(key_list[1], (SEQUENCE_TOKENS, D), 1.0, 6.0, ((0, 128),))
    value_rows = gaussian(key_list[2], (SEQUENCE_TOKENS, D), 1.0, 6.0, ((0, 128),))
    gate_logits = gaussian(key_list[3], (SEQUENCE_TOKENS, D), 1.0, 6.0, ((0, 128),))
    residual_in = gaussian(key_list[4], (SEQUENCE_TOKENS, D), 1.0, 6.0, ((0, 128),))
    decay_rate = draw_decay_rate(jax.random.fold_in(key_list[12], 71), 0)
    attention_gain = jnp.clip(1.0 + 0.15 * jax.random.normal(key_list[6], (D,), jnp.float32), 0.25, 1.75)
    expert_gain = jnp.clip(1.0 + 0.15 * jax.random.normal(key_list[7], (D,), jnp.float32), 0.25, 1.75)
    expert_index_keys = jax.random.split(jax.random.fold_in(key_list[8], 1), SEQUENCE_TOKENS // TOK_DEV)
    expert_index_turns = jax.random.permutation(jax.random.fold_in(key_list[8], 3), SEQUENCE_TOKENS // TOK_DEV)
    expert_index = jax.vmap(lambda own, number: routed_block(jax.random.fold_in(key_list[8], 2), own, number, TOK_DEV, EXPERTS, TOP, CAP, 2))(expert_index_keys, expert_index_turns).reshape((SEQUENCE_TOKENS, TOP))
    router_weight = jnp.clip(0.1 + 0.79999997 * jax.random.uniform(key_list[9], (SEQUENCE_TOKENS, TOP), jnp.float32) ** block_scale(key_list[9], (SEQUENCE_TOKENS, TOP), ((0, 128),), -0.2, 0.2), 0.1, 0.9)
    gate_up_weight = gaussian(key_list[10], (EXPERTS, D, 2, FF), D ** -0.5, 0.09375, ((0, 16), (3, 8)))
    down_weight = gaussian(key_list[11], (EXPERTS, FF, D), FF ** -0.5, 0.09375, ((0, 16), (1, 8)))
    return dict(queries=queries, key_rows=key_rows, value_rows=value_rows, gate_logits=gate_logits, residual_in=residual_in, decay_rate=decay_rate, attention_gain=attention_gain, expert_gain=expert_gain, expert_index=expert_index, router_weight=router_weight, gate_up_weight=gate_up_weight, down_weight=down_weight)


def block_terms(query_heads, key_heads, value_heads, rates):
    token_count = rates.shape[0]
    running = jnp.cumsum(rates, axis=0)
    running_rows = running.T
    spacing = running_rows[:, :, None] - running_rows[:, None, :]
    positions = lax.iota(jnp.int32, token_count)
    causal = (positions[:, None] >= positions[None, :])[None]
    fading = jnp.where(causal, jnp.exp(-jnp.where(causal, spacing, 0.0)), 0.0)
    scores = jnp.einsum('thd,shd->hts', query_heads.astype(jnp.float32), key_heads.astype(jnp.float32), precision=lax.Precision.HIGHEST)
    weights = (scores * fading).astype(jnp.bfloat16)
    local_out = jnp.einsum('hts,shd->thd', weights.astype(jnp.float32), value_heads.astype(jnp.float32), precision=lax.Precision.HIGHEST)
    block_end = running[-1]
    key_faded = (key_heads.astype(jnp.float32) * jnp.exp(-(block_end[None, :] - running))[:, :, None]).astype(jnp.bfloat16)
    local_state = jnp.einsum('thd,the->hde', key_faded.astype(jnp.float32), value_heads.astype(jnp.float32), precision=lax.Precision.HIGHEST)
    return (local_out, local_state, jnp.exp(-block_end), running)

def reference(queries, key_rows, value_rows, gate_logits, residual_in, decay_rate, attention_gain, expert_gain, expert_index, router_weight, gate_up_weight, down_weight):
    block_total = SEQUENCE_TOKENS // TOK_DEV
    query_blocks = queries.reshape(block_total, TOK_DEV, ATTENTION_HEADS, HEAD)
    key_blocks = key_rows.reshape(block_total, TOK_DEV, ATTENTION_HEADS, HEAD)
    value_blocks = value_rows.reshape(block_total, TOK_DEV, ATTENTION_HEADS, HEAD)
    rate_blocks = decay_rate.reshape(block_total, TOK_DEV, ATTENTION_HEADS)

    def advance(incoming, blocks):
        query_heads, key_heads, value_heads, rates = blocks
        local_out, local_state, block_keep, running = block_terms(query_heads, key_heads, value_heads, rates)
        carried_low = incoming.astype(jnp.bfloat16).astype(jnp.float32)
        carried_out = jnp.exp(-running)[:, :, None] * jnp.einsum('thd,hde->the', query_heads.astype(jnp.float32), carried_low, precision=lax.Precision.HIGHEST)
        updated = block_keep[:, None, None] * incoming + local_state
        return (updated, local_out + carried_out)
    start_state = jnp.zeros((ATTENTION_HEADS, HEAD, HEAD), jnp.float32)
    final_state, attention = lax.scan(advance, start_state, (query_blocks, key_blocks, value_blocks, rate_blocks))
    attention = attention.reshape(SEQUENCE_TOKENS, D)
    inv_norm = lax.rsqrt(lax.optimization_barrier(jnp.mean(attention * attention, axis=1, keepdims=True)) + 1e-05)
    stream = (residual_in.astype(jnp.float32) + attention * inv_norm * attention_gain * jax.nn.sigmoid(gate_logits.astype(jnp.float32))).astype(jnp.bfloat16)
    stream_wide = stream.astype(jnp.float32)
    inv_stream = lax.rsqrt(lax.optimization_barrier(jnp.mean(stream_wide * stream_wide, axis=1, keepdims=True)) + 1e-05)
    expert_input = (stream_wide * inv_stream * expert_gain).astype(jnp.bfloat16)
    flat_choice = expert_index.reshape(-1)
    order = jnp.argsort(flat_choice, stable=True).astype(jnp.int32)
    per_expert = SEQUENCE_TOKENS * TOP // EXPERTS
    token_list = (order // TOP).astype(jnp.int32).reshape(EXPERTS, per_expert)

    def one_expert(operands):
        token_ids, gate_up, down_all = operands
        token_input = expert_input[token_ids]
        expert_sum = jnp.zeros((per_expert, D), jnp.float32)
        for block_index in range(N_GRP):
            lower = block_index * HBLK
            gate_up_block = gate_up[:, :, lower:lower + HBLK].reshape(D, 2 * HBLK)
            pair = jnp.dot(token_input, gate_up_block, preferred_element_type=jnp.float32).reshape(per_expert, 2, HBLK)
            hidden = (jax.nn.silu(pair[:, 0]) * pair[:, 1]).astype(jnp.bfloat16)
            partial_value = jnp.dot(hidden, down_all[lower:lower + HBLK], preferred_element_type=jnp.float32).astype(jnp.bfloat16)
            partial_value = lax.optimization_barrier(partial_value)
            expert_sum = expert_sum + partial_value.astype(jnp.float32)
        return expert_sum.astype(jnp.bfloat16)
    expert_out = lax.map(one_expert, (token_list, gate_up_weight, down_weight))
    sorted_weight = router_weight.reshape(-1)[order].reshape(EXPERTS, per_expert)
    weighted = (sorted_weight[:, :, None] * expert_out.astype(jnp.float32)).reshape(-1, D)
    mixed = jnp.zeros((SEQUENCE_TOKENS, D), jnp.float32).at[token_list.reshape(-1)].add(weighted)
    return (stream_wide + mixed).astype(jnp.bfloat16)
```

```python
import functools

import jax
import jax.numpy as jnp
from jax import lax
from jax.experimental import pallas as pl
from jax.experimental.pallas import tpu as pltpu
from jax.sharding import PartitionSpec as P

F32, BF16 = (jnp.float32, jnp.bfloat16)
HEAD = 128
PIECE = 32
EXTRA = 16
MIB = 1 << 20
NT = (((1,), (1,)), ((), ()))
TN = (((0,), (0,)), ((), ()))


def vmem(count):
    return [pl.BlockSpec(memory_space=pltpu.VMEM)] * count


def whole_call(kernel, outs, args, flops, limit, scratch=()):
    moved = sum(a.size * a.dtype.itemsize for a in (*args, *outs))
    return pl.pallas_call(
        kernel,
        out_shape=outs,
        in_specs=vmem(len(args)),
        out_specs=vmem(len(outs)),
        scratch_shapes=list(scratch),
        cost_estimate=pl.CostEstimate(flops=flops, bytes_accessed=moved, transcendentals=0),
        compiler_params=pltpu.CompilerParams(vmem_limit_bytes=limit * MIB),
    )(*args)


def lane_block(h):
    return slice(h * HEAD, (h + 1) * HEAD)


def state_kernel(rates_ref, key_ref, value_ref, sent_ref, by_head_ref, by_token_ref):
    heads, tokens = rates_ref.shape
    at = lambda dim: lax.broadcasted_iota(jnp.int32, (tokens, tokens), dim)
    upto = (at(0) <= at(1)).astype(F32)
    by_head = jnp.dot(
        rates_ref[...], upto, precision=lax.Precision.HIGHEST, preferred_element_type=F32
    )
    by_token = by_head.T
    by_head_ref[...] = by_head
    by_token_ref[...] = by_token
    fade = jnp.exp(by_token - by_token[tokens - 1 :, :])
    keep = jnp.broadcast_to(jnp.exp(-by_head[:, tokens - 1 :]), (heads, HEAD))
    high = keep.astype(BF16).astype(F32)
    middle = (keep - high).astype(BF16).astype(F32)
    low = keep - high - middle
    row = lax.broadcasted_iota(jnp.int32, (EXTRA, HEAD), 0)
    parts = HEAD // PIECE
    for h in range(heads):
        faded = (key_ref[:, lane_block(h)].astype(F32) * fade[:, h : h + 1]).astype(BF16)
        state = lax.dot_general(faded, value_ref[:, lane_block(h)], TN, preferred_element_type=F32)
        tail = jnp.where(row == 0, high[h : h + 1], 0.0)
        tail = jnp.where(row == 1, middle[h : h + 1], tail)
        tail = jnp.where(row == 2, low[h : h + 1], tail).astype(BF16)
        for part in range(parts):
            sent_ref[h * parts + part, :PIECE, :] = state[
                part * PIECE : (part + 1) * PIECE
            ].astype(BF16)
            sent_ref[h * parts + part, PIECE:, :] = tail


def scan_kernel(arrived_ref, carried_ref):
    def step(block, carry):
        carried_ref[block] = carry.astype(BF16)
        tail = arrived_ref[block, PIECE:, :].astype(F32)
        keep = tail[0:1] + tail[1:2] + tail[2:3]
        return keep * carry + arrived_ref[block, :PIECE, :].astype(F32)

    lax.fori_loop(
        0, carried_ref.shape[0], step, jnp.zeros((PIECE, HEAD), F32), unroll=8
    )


def local_kernel(query_ref, key_ref, value_ref, by_head_ref, by_token_ref, out_ref):
    heads, tokens = by_head_ref.shape
    at = lambda dim: lax.broadcasted_iota(jnp.int32, (tokens, tokens), dim)
    causal = at(0) >= at(1)
    for h in range(heads):
        scores = lax.dot_general(
            query_ref[:, lane_block(h)], key_ref[:, lane_block(h)], NT, preferred_element_type=F32
        )
        spacing = by_head_ref[h : h + 1, :] - by_token_ref[:, h : h + 1]
        fading = jnp.exp(jnp.minimum(spacing, 0.0))
        weights = jnp.where(causal, scores * fading, 0.0).astype(BF16)
        out_ref[:, lane_block(h)] = jnp.dot(
            weights, value_ref[:, lane_block(h)], preferred_element_type=F32
        )


def places(index_ref, experts):
    tokens = index_ref.shape[1]
    expert = lax.broadcasted_iota(jnp.int32, (experts, tokens), 0)
    first, second = (index_ref[0:1, :] == expert, index_ref[1:2, :] == expert)
    named = (first | second).astype(F32)
    at = lambda dim: lax.broadcasted_iota(jnp.int32, (tokens, tokens), dim)
    earlier = (at(0) < at(1)).astype(BF16)
    slot = jnp.dot(named.astype(BF16), earlier, preferred_element_type=F32)
    return first, second, jnp.where(named > 0.0, slot, -1.0)


def chunk_rows(slot, chunk, rows):
    experts, tokens = slot.shape
    wanted = lax.broadcasted_iota(jnp.int32, (rows, tokens), 0).astype(F32) + float(chunk * rows)
    return [slot[e : e + 1, :] == wanted for e in range(experts)]


def stream_kernel(
    query_ref,
    carried_ref,
    by_token_ref,
    local_ref,
    gate_ref,
    residual_ref,
    attention_gain_ref,
    expert_gain_ref,
    index_ref,
    stream_ref,
    *rest,
):
    *bin_refs, attention_ref = rest
    tokens, width = query_ref.shape
    heads = width // HEAD
    since = jnp.exp(-by_token_ref[...])
    total = jnp.zeros((tokens, HEAD), F32)
    for h in range(heads):
        carried_out = jnp.dot(
            query_ref[:, lane_block(h)], carried_ref[h], preferred_element_type=F32
        )
        attention = local_ref[:, lane_block(h)] + since[:, h : h + 1] * carried_out
        attention_ref[:, lane_block(h)] = attention
        total = total + attention * attention
    inverse = lax.rsqrt(jnp.sum(total, axis=1, keepdims=True) / width + 1e-05)
    total = jnp.zeros((tokens, HEAD), F32)
    for h in range(heads):
        gate = gate_ref[:, lane_block(h)].astype(F32)
        sigmoid = 1.0 / (1.0 + jnp.exp(-gate))
        gained = attention_ref[:, lane_block(h)] * inverse * attention_gain_ref[:, lane_block(h)]
        stream = (residual_ref[:, lane_block(h)].astype(F32) + gained * sigmoid).astype(BF16)
        stream_ref[:, lane_block(h)] = stream
        wide = stream.astype(F32)
        total = total + wide * wide
    inverse = lax.rsqrt(jnp.sum(total, axis=1, keepdims=True) / width + 1e-05)
    experts = bin_refs[0].shape[0]
    rows = bin_refs[0].shape[1]
    slot = places(index_ref, experts)[2]
    selectors = [
        jnp.concatenate([m.astype(F32) for m in chunk_rows(slot, c, rows)], axis=0).astype(BF16)
        for c in range(len(bin_refs))
    ]
    for h in range(heads):
        wide = stream_ref[:, lane_block(h)].astype(F32)
        entry = (wide * inverse * expert_gain_ref[:, lane_block(h)]).astype(BF16)
        for selector, bin_ref in zip(selectors, bin_refs):
            picked = jnp.dot(selector, entry, preferred_element_type=F32)
            bin_ref[:, :, lane_block(h)] = picked.astype(BF16).reshape(experts, rows, HEAD)


def mix_kernel(stream_ref, index_ref, router_ref, *rest):
    *returned_refs, out_ref = rest
    experts, rows, width = returned_refs[0].shape
    first, second, slot = places(index_ref, experts)
    scale = jnp.where(first, router_ref[0:1, :], 0.0) + jnp.where(second, router_ref[1:2, :], 0.0)
    weights = []
    for c in range(len(returned_refs)):
        masks = chunk_rows(slot, c, rows)
        chosen = jnp.concatenate(
            [jnp.where(m, scale[e : e + 1, :], 0.0) for e, m in enumerate(masks)], axis=0
        ).T
        high = chosen.astype(BF16)
        weights.append((high, (chosen - high.astype(F32)).astype(BF16)))
    for h in range(width // HEAD // 4):
        columns = slice(h * 4 * HEAD, (h + 1) * 4 * HEAD)
        total = stream_ref[:, columns].astype(F32)
        for (high, low), returned_ref in zip(weights, returned_refs):
            returned = returned_ref[:, :, columns].reshape(experts * rows, 4 * HEAD)
            total = total + jnp.dot(high, returned, preferred_element_type=F32)
            total = total + jnp.dot(low, returned, preferred_element_type=F32)
        out_ref[:, columns] = total.astype(BF16)


def expert_kernel(
    steps_in,
    steps_out,
    own_ref,
    left_ref,
    right_ref,
    far_a_ref,
    far_b_ref,
    up_own_ref,
    up_other_ref,
    down_own_ref,
    down_other_ref,
    out_own_ref,
    out_left_ref,
    out_right_ref,
    out_far_ref,
    rows_ref,
    turned_ref,
    hidden_own_ref,
    hidden_other_ref,
):
    step = pl.program_id(0)
    half = steps_in // 2
    count = own_ref.shape[0]

    @pl.when(step == 0)
    def _():
        rows_ref[0:count] = own_ref[...]
        rows_ref[count : 2 * count] = left_ref[...]
        rows_ref[2 * count : 3 * count] = right_ref[...]
        rows_ref[3 * count : 3 * count + count // 2] = far_a_ref[...]
        rows_ref[3 * count + count // 2 :] = far_b_ref[...]

    def enter(weight_ref):
        tile = weight_ref.shape[1]
        gate = lax.dot_general(weight_ref[0], rows_ref[...], NT, preferred_element_type=F32)
        up = lax.dot_general(weight_ref[1], rows_ref[...], NT, preferred_element_type=F32)
        hidden = gate / (1.0 + jnp.exp(-gate)) * up
        turned_ref[pl.ds(pl.multiple_of(step * tile, tile), tile), :] = hidden.astype(BF16)

    @pl.when(step < half)
    def _():
        enter(up_own_ref)

    @pl.when((step >= half) & (step < steps_in))
    def _():
        enter(up_other_ref)

    @pl.when(step == steps_in)
    def _():
        units = hidden_own_ref.shape[1]
        hidden_own_ref[...] = turned_ref[:units, :].T
        hidden_other_ref[...] = turned_ref[units:, :].T

    @pl.when(step >= steps_in)
    def _():
        out = jnp.dot(hidden_own_ref[...], down_own_ref[...], preferred_element_type=F32)
        out = out + jnp.dot(hidden_other_ref[...], down_other_ref[...], preferred_element_type=F32)
        out = out.astype(BF16)
        for place, ref in enumerate((out_own_ref, out_left_ref, out_right_ref, out_far_ref)):
            ref[...] = out[place * count : (place + 1) * count]


def expert_rows(blocks, up_own, up_other, down_own, down_other):
    count, width = blocks[0].shape
    units = down_own.shape[0]
    steps_in, steps_out = (4, 4)
    tile, columns = (2 * units // steps_in, width // steps_out)
    half = steps_in // 2
    once = pl.Buffered(1)
    fixed = lambda a: pl.BlockSpec(a.shape, lambda i: (0, 0), pipeline_mode=once)
    clip = lambda i, low, high: jnp.minimum(jnp.maximum(i, low), high)
    up_spec = lambda start: pl.BlockSpec(
        (2, tile, width), lambda i: (0, clip(i - start, 0, half - 1), 0)
    )
    down_spec = pl.BlockSpec((units, columns), lambda i: (0, clip(i - steps_in, 0, steps_out - 1)))
    out_spec = pl.BlockSpec((count, columns), lambda i: (0, clip(i - steps_in, 0, steps_out - 1)))
    return pl.pallas_call(
        functools.partial(expert_kernel, steps_in, steps_out),
        grid=(steps_in + steps_out,),
        in_specs=[fixed(b) for b in blocks]
        + [up_spec(0), up_spec(half), down_spec, down_spec],
        out_specs=[out_spec] * 4,
        out_shape=[jax.ShapeDtypeStruct((count, width), BF16)] * 4,
        scratch_shapes=[
            pltpu.VMEM((4 * count, width), BF16),
            pltpu.VMEM((2 * units, 4 * count), BF16),
            pltpu.VMEM((4 * count, units), BF16),
            pltpu.VMEM((4 * count, units), BF16),
        ],
        cost_estimate=pl.CostEstimate(
            flops=4 * count * 2 * units * width * 6,
            bytes_accessed=6 * units * width * 2 + 8 * count * width * 2,
            transcendentals=0,
        ),
        compiler_params=pltpu.CompilerParams(vmem_limit_bytes=44 * MIB),
    )(*blocks, up_own, up_other, down_own, down_other)


def body(
    queries,
    key_rows,
    value_rows,
    gate_logits,
    residual_in,
    decay_rate,
    attention_gain,
    expert_gain,
    expert_index,
    router_weight,
    gate_up_weight,
    down_weight,
):
    groups, experts = (lax.axis_size("grp"), lax.axis_size("seq"))
    devices = groups * experts
    tokens, width = queries.shape
    heads = decay_rate.shape[1]
    chunks = 2
    slots = tokens * expert_index.shape[1] // experts
    rows = slots // chunks
    count = experts * rows

    swap = [(g, g ^ 1) for g in range(groups)]
    ahead = [(g, (g + 2) % groups) for g in range(groups)]
    back = [(g, (g - 2) % groups) for g in range(groups)]
    go_ahead = lambda a: lax.ppermute(a, "grp", ahead)
    go_back = lambda a: lax.ppermute(a, "grp", back)
    everywhere = ("grp", "seq")
    exchange = lambda a, axis: lax.all_to_all(a, axis, split_axis=0, concat_axis=0, tiled=True)
    shape = jax.ShapeDtypeStruct

    up_own = jnp.transpose(gate_up_weight[0], (1, 2, 0))
    down_own = down_weight[0]
    up_other = lax.ppermute(up_own, "grp", swap)
    down_other = lax.ppermute(down_own, "grp", swap)

    sent, by_head, by_token = whole_call(
        state_kernel,
        [
            shape((devices, PIECE + EXTRA, HEAD), BF16),
            shape((heads, tokens), F32),
            shape((tokens, heads), F32),
        ],
        [decay_rate.T, key_rows, value_rows],
        2 * tokens * width * HEAD,
        16,
    )
    arrived = exchange(sent, everywhere)
    (local_out,) = whole_call(
        local_kernel,
        [shape((tokens, width), F32)],
        [queries, key_rows, value_rows, by_head, by_token],
        4 * tokens * width * tokens,
        16,
    )
    (carried,) = whole_call(
        scan_kernel, [shape((devices, PIECE, HEAD), BF16)], [arrived], devices * PIECE * HEAD, 16
    )
    carried_low = exchange(carried, everywhere).reshape(heads, HEAD, HEAD)
    index = expert_index.T
    stream, *bins = whole_call(
        stream_kernel,
        [shape((tokens, width), BF16)] + [shape((experts, rows, width), BF16)] * chunks,
        [
            queries,
            carried_low,
            by_token,
            local_out,
            gate_logits,
            residual_in,
            attention_gain[None, :],
            expert_gain[None, :],
            index,
        ],
        2 * tokens * width * (HEAD + chunks * count),
        32,
        [pltpu.VMEM((tokens, width), F32)],
    )

    half = count // 2
    returned = []
    for bin_rows in bins:
        own = exchange(bin_rows, "seq").reshape(count, width)
        left, right = (go_ahead(own), go_back(own))
        far_a, far_b = (go_ahead(left[:half]), go_back(right[half:]))
        out_own, out_left, out_right, out_far = expert_rows(
            (own, left, right, far_a, far_b), up_own, up_other, down_own, down_other
        )
        pass_a, pass_b = (go_ahead(out_far[:half]), go_back(out_far[half:]))
        right_low, left_high = (go_ahead(out_right[half:]), go_back(out_left[:half]))
        wide = lambda a: a.astype(F32)
        right_high = go_ahead((wide(out_right[:half]) + wide(pass_a)).astype(BF16))
        left_low = go_back((wide(out_left[half:]) + wide(pass_b)).astype(BF16))
        summed = jnp.concatenate(
            [
                wide(out_own[:half]) + wide(right_high) + wide(left_high),
                wide(out_own[half:]) + wide(right_low) + wide(left_low),
            ],
            axis=0,
        ).astype(BF16)
        returned.append(exchange(summed.reshape(experts, rows, width), "seq"))
    (out,) = whole_call(
        mix_kernel,
        [shape((tokens, width), BF16)],
        [stream, index, router_weight.T, *returned],
        4 * tokens * width * count * chunks,
        16,
    )
    return out


def solution(mesh):
    rows = P(("grp", "seq"), None)
    return jax.shard_map(
        body,
        mesh=mesh,
        in_specs=(
            rows,
            rows,
            rows,
            rows,
            rows,
            rows,
            P(),
            P(),
            rows,
            rows,
            P("seq", None, None, "grp"),
            P("seq", "grp", None),
        ),
        out_specs=rows,
        check_vma=False,
    )
```

```python
import functools

import jax
import jax.numpy as jnp
from jax import lax
from jax.experimental import pallas as pl
from jax.experimental.pallas import tpu as pltpu
from jax.sharding import Mesh
from jax.sharding import PartitionSpec as P

F32, BF16 = (jnp.float32, jnp.bfloat16)
HEAD = 128
EXTRA = 8
MIB = 1 << 20
NT = (((1,), (1,)), ((), ()))
TN = (((0,), (0,)), ((), ()))


def vmem(count):
    return [pl.BlockSpec(memory_space=pltpu.VMEM)] * count


def whole_call(kernel, outs, args, flops, limit, scratch=(), in_place=()):
    moved = sum(a.size * a.dtype.itemsize for a in (*args, *outs))
    return pl.pallas_call(
        kernel,
        out_shape=outs,
        in_specs=[
            pl.BlockSpec(memory_space=pltpu.HBM if place in in_place else pltpu.VMEM)
            for place in range(len(args))
        ],
        out_specs=vmem(len(outs)),
        scratch_shapes=list(scratch),
        cost_estimate=pl.CostEstimate(flops=flops, bytes_accessed=moved, transcendentals=0),
        compiler_params=pltpu.CompilerParams(vmem_limit_bytes=limit * MIB),
    )(*args)


def lane_block(h):
    return slice(h * HEAD, (h + 1) * HEAD)


def state_kernel(
    rates_in_ref,
    key_rows_ref,
    value_rows_ref,
    sent_ref,
    by_head_ref,
    by_token_ref,
    rates_ref,
    key_ref,
    value_ref,
    loaded,
    rates_loaded,
):
    heads, tokens = rates_ref.shape
    rates_copy = pltpu.make_async_copy(rates_in_ref, rates_ref, rates_loaded)
    rates_copy.start()
    groups = loaded.shape[1]
    columns = heads * HEAD // groups
    copies = [
        [
            pltpu.make_async_copy(
                source.at[:, pl.ds(g * columns, columns)],
                target.at[:, pl.ds(g * columns, columns)],
                loaded.at[place, g],
            )
            for place, (source, target) in enumerate(
                ((key_rows_ref, key_ref), (value_rows_ref, value_ref))
            )
        ]
        for g in range(groups)
    ]
    for pair in copies:
        for copy in pair:
            copy.start()
    rates_copy.wait()
    at = lambda dim: lax.broadcasted_iota(jnp.int32, (tokens, tokens), dim)
    upto = (at(0) <= at(1)).astype(F32)
    by_head = jnp.dot(
        rates_ref[...], upto, precision=lax.Precision.HIGHEST, preferred_element_type=F32
    )
    by_token = by_head.T
    by_head_ref[...] = by_head
    by_token_ref[...] = by_token
    fade = jnp.exp(by_token - by_token[tokens - 1 :, :])
    keep = jnp.broadcast_to(jnp.exp(-by_head[:, tokens - 1 :]), (heads, HEAD))
    high = keep.astype(BF16).astype(F32)
    middle = (keep - high).astype(BF16).astype(F32)
    low = keep - high - middle
    row = lax.broadcasted_iota(jnp.int32, (EXTRA, HEAD), 0)
    for h in range(heads):
        if h % (heads // groups) == 0:
            for copy in copies[h // (heads // groups)]:
                copy.wait()
        faded = (key_ref[:, lane_block(h)].astype(F32) * fade[:, h : h + 1]).astype(BF16)
        state = lax.dot_general(faded, value_ref[:, lane_block(h)], TN, preferred_element_type=F32)
        tail = jnp.where(row == 0, high[h : h + 1], 0.0)
        tail = jnp.where(row == 1, middle[h : h + 1], tail)
        tail = jnp.where(row == 2, low[h : h + 1], tail).astype(BF16)
        sent_ref[h, :HEAD, :] = state.astype(BF16)
        sent_ref[h, HEAD:, :] = tail


def scan_kernel(arrived_ref, within_ref, kept_ref, total_ref):
    def step(block, carry):
        state, kept = carry
        within_ref[block] = state
        kept_ref[block] = kept
        tail = arrived_ref[block, HEAD:, :].astype(F32)
        keep = tail[0:1] + tail[1:2] + tail[2:3]
        return keep * state + arrived_ref[block, :HEAD, :].astype(F32), keep * kept

    start = (jnp.zeros((HEAD, HEAD), F32), jnp.ones((EXTRA, HEAD), F32))
    state, kept = lax.fori_loop(0, within_ref.shape[0], step, start, unroll=4)
    total_ref[:HEAD, :] = state
    total_ref[HEAD:, :] = kept


def carry_kernel(within_ref, kept_ref, *rest):
    *total_refs, carried_ref = rest
    before = jnp.zeros((HEAD, HEAD), F32)
    for total_ref in reversed(total_refs):
        before = total_ref[:HEAD, :] + total_ref[HEAD : HEAD + 1, :] * before

    def step(block, _):
        carried = within_ref[block] + kept_ref[block, 0:1, :] * before
        carried_ref[block] = carried.astype(BF16)
        return 0

    lax.fori_loop(0, carried_ref.shape[0], step, 0, unroll=4)


def local_kernel(
    query_ref,
    key_ref,
    value_ref,
    by_head_ref,
    by_token_ref,
    out_ref,
):
    heads, tokens = by_head_ref.shape
    at = lambda dim: lax.broadcasted_iota(jnp.int32, (tokens, tokens), dim)
    causal = at(0) >= at(1)
    for h in range(heads):
        scores = lax.dot_general(
            query_ref[:, lane_block(h)], key_ref[:, lane_block(h)], NT, preferred_element_type=F32
        )
        spacing = by_head_ref[h : h + 1, :] - by_token_ref[:, h : h + 1]
        fading = jnp.exp(jnp.minimum(spacing, 0.0))
        weights = jnp.where(causal, scores * fading, 0.0).astype(BF16)
        out_ref[:, lane_block(h)] = jnp.dot(
            weights, value_ref[:, lane_block(h)], preferred_element_type=F32
        )


def places(index_ref, experts):
    tokens = index_ref.shape[1]
    expert = lax.broadcasted_iota(jnp.int32, (experts, tokens), 0)
    first, second = (index_ref[0:1, :] == expert, index_ref[1:2, :] == expert)
    named = (first | second).astype(F32)
    at = lambda dim: lax.broadcasted_iota(jnp.int32, (tokens, tokens), dim)
    earlier = (at(0) < at(1)).astype(BF16)
    slot = jnp.dot(named.astype(BF16), earlier, preferred_element_type=F32)
    return first, second, jnp.where(named > 0.0, slot, -1.0)


def chunk_rows(slot, chunk, rows):
    experts, tokens = slot.shape
    wanted = lax.broadcasted_iota(jnp.int32, (rows, tokens), 0).astype(F32) + float(chunk * rows)
    return [slot[e : e + 1, :] == wanted for e in range(experts)]


def stream_kernel(
    query_ref,
    local_ref,
    gate_ref,
    residual_ref,
    carried_ref,
    by_token_ref,
    attention_gain_ref,
    expert_gain_ref,
    index_ref,
    stream_ref,
    *rest,
):
    *bin_refs, attention_ref = rest
    tokens, width = query_ref.shape
    heads = width // HEAD
    since = jnp.exp(-by_token_ref[...])
    total = jnp.zeros((tokens, HEAD), F32)
    for h in range(heads):
        carried_out = jnp.dot(
            query_ref[:, lane_block(h)], carried_ref[h], preferred_element_type=F32
        )
        attention = local_ref[:, lane_block(h)] + since[:, h : h + 1] * carried_out
        attention_ref[:, lane_block(h)] = attention
        total = total + attention * attention
    inverse = lax.rsqrt(jnp.sum(total, axis=1, keepdims=True) / width + 1e-05)
    total = jnp.zeros((tokens, HEAD), F32)
    for h in range(heads):
        gate = gate_ref[:, lane_block(h)].astype(F32)
        gain = attention_gain_ref[:, lane_block(h)] / (1.0 + jnp.exp(-gate))
        gated = attention_ref[:, lane_block(h)] * inverse * gain
        stream = (residual_ref[:, lane_block(h)].astype(F32) + gated).astype(BF16)
        stream_ref[:, lane_block(h)] = stream
        wide = stream.astype(F32)
        total = total + wide * wide
    inverse = lax.rsqrt(jnp.sum(total, axis=1, keepdims=True) / width + 1e-05)
    experts = bin_refs[0].shape[0]
    rows = bin_refs[0].shape[1]
    slot = places(index_ref, experts)[2]
    selectors = [
        jnp.concatenate([m.astype(F32) for m in chunk_rows(slot, c, rows)], axis=0).astype(BF16)
        for c in range(len(bin_refs))
    ]
    for h in range(heads):
        wide = stream_ref[:, lane_block(h)].astype(F32)
        entry = (wide * inverse * expert_gain_ref[:, lane_block(h)]).astype(BF16)
        for selector, bin_ref in zip(selectors, bin_refs):
            picked = jnp.dot(selector, entry, preferred_element_type=F32)
            bin_ref[:, :, lane_block(h)] = picked.astype(BF16).reshape(experts, rows, HEAD)


def mix_kernel(stream_ref, index_ref, router_ref, *rest):
    *returned_refs, out_ref = rest
    experts, rows, width = returned_refs[0].shape
    first, second, slot = places(index_ref, experts)
    scale = jnp.where(first, router_ref[0:1, :], 0.0) + jnp.where(second, router_ref[1:2, :], 0.0)
    weights = []
    for c in range(len(returned_refs)):
        masks = chunk_rows(slot, c, rows)
        chosen = jnp.concatenate(
            [jnp.where(m, scale[e : e + 1, :], 0.0) for e, m in enumerate(masks)], axis=0
        ).T
        high = chosen.astype(BF16)
        weights.append((high, (chosen - high.astype(F32)).astype(BF16)))
    for h in range(width // HEAD // 4):
        columns = slice(h * 4 * HEAD, (h + 1) * 4 * HEAD)
        total = stream_ref[:, columns].astype(F32)
        for (high, low), returned_ref in zip(weights, returned_refs):
            returned = returned_ref[:, :, columns].reshape(experts * rows, 4 * HEAD)
            total = total + jnp.dot(high, returned, preferred_element_type=F32)
            total = total + jnp.dot(low, returned, preferred_element_type=F32)
        out_ref[:, columns] = total.astype(BF16)


def expert_kernel(
    own_ref,
    left_ref,
    right_ref,
    far_ref,
    up_own_ref,
    up_other_ref,
    down_own_ref,
    down_other_ref,
    out_own_ref,
    out_left_ref,
    out_right_ref,
    out_far_ref,
    rows_ref,
    up_ref,
    down_ref,
    turned_ref,
    hidden_ref,
    up_sem,
    down_sem,
):
    count = own_ref.shape[0]
    tiles, _, tile, width = up_ref.shape
    units = down_own_ref.shape[0]
    parts, _, columns = down_ref.shape
    each = tiles // 2

    def up_copies(k):
        source = (up_own_ref, up_other_ref)[k // each]
        part = source.at[:, pl.ds(k % each * tile, tile), :]
        return [pltpu.make_async_copy(part, up_ref.at[k], up_sem.at[k])]

    def down_copies(k):
        return [
            pltpu.make_async_copy(
                source.at[:, pl.ds(k * columns, columns)],
                down_ref.at[k, pl.ds(place * units, units), :],
                down_sem.at[k, place],
            )
            for place, source in enumerate((down_own_ref, down_other_ref))
        ]

    loads = [up_copies(k) for k in range(tiles)] + [down_copies(k) for k in range(parts)]
    in_flight = 2

    def start(k):
        if k < len(loads):
            for copy in loads[k]:
                copy.start()

    def arrive(k):
        for copy in loads[k]:
            copy.wait()
        start(k + in_flight)

    for k in range(in_flight):
        start(k)
    rows_ref[0:count] = own_ref[...]
    rows_ref[count : 2 * count] = left_ref[...]
    rows_ref[2 * count : 3 * count] = right_ref[...]
    rows_ref[3 * count :] = far_ref[...]
    for k in range(tiles):
        arrive(k)
        both = up_ref[k].reshape(2 * tile, width)
        pair = lax.dot_general(both, rows_ref[...], NT, preferred_element_type=F32)
        gate, up = (pair[:tile], pair[tile:])
        hidden = gate / (1.0 + jnp.exp(-gate)) * up
        turned_ref[k * tile : (k + 1) * tile, :] = hidden.astype(BF16)
    hidden_ref[...] = turned_ref[...].T
    for k in range(parts):
        arrive(tiles + k)
        out = jnp.dot(hidden_ref[...], down_ref[k], preferred_element_type=F32).astype(BF16)
        for place, ref in enumerate((out_own_ref, out_left_ref, out_right_ref, out_far_ref)):
            ref[:, k * columns : (k + 1) * columns] = out[place * count : (place + 1) * count]


def expert_rows(blocks, up_own, up_other, down_own, down_other):
    count, width = blocks[0].shape
    units = down_own.shape[0]
    tiles, parts = (4, 4)
    tile, columns = (2 * units // tiles, width // parts)
    in_place = [pl.BlockSpec(memory_space=pltpu.HBM)] * 4
    return pl.pallas_call(
        expert_kernel,
        in_specs=vmem(len(blocks)) + in_place,
        out_specs=vmem(4),
        out_shape=[jax.ShapeDtypeStruct((count, width), BF16)] * 4,
        scratch_shapes=[
            pltpu.VMEM((4 * count, width), BF16),
            pltpu.VMEM((tiles, 2, tile, width), BF16),
            pltpu.VMEM((parts, 2 * units, columns), BF16),
            pltpu.VMEM((2 * units, 4 * count), BF16),
            pltpu.VMEM((4 * count, 2 * units), BF16),
            pltpu.SemaphoreType.DMA((tiles,)),
            pltpu.SemaphoreType.DMA((parts, 2)),
        ],
        cost_estimate=pl.CostEstimate(
            flops=4 * count * 2 * units * width * 6,
            bytes_accessed=6 * units * width * 2 + 8 * count * width * 2,
            transcendentals=0,
        ),
        compiler_params=pltpu.CompilerParams(vmem_limit_bytes=46 * MIB),
    )(*blocks, up_own, up_other, down_own, down_other)


def body(
    queries,
    key_rows,
    value_rows,
    gate_logits,
    residual_in,
    decay_rate,
    attention_gain,
    expert_gain,
    expert_index,
    router_weight,
    gate_up_weight,
    down_weight,
):
    chips, experts = (lax.axis_size("x"), lax.axis_size("seq"))
    tokens, width = queries.shape
    heads = decay_rate.shape[1]
    chunks = 2
    slots = tokens * expert_index.shape[1] // experts
    rows = slots // chunks
    count = experts * rows

    swap = lambda a: lax.ppermute(a, "core", [(0, 1), (1, 0)])
    go_ahead = lambda a: lax.ppermute(a, "x", [(i, (i + 1) % chips) for i in range(chips)])
    go_back = lambda a: lax.ppermute(a, "x", [(i, (i - 1) % chips) for i in range(chips)])
    to_later = lambda a, k: lax.ppermute(a, "x", [(i, i + k) for i in range(chips - k)])
    plane = ("core", "seq")
    after = lambda value, *earlier: lax.optimization_barrier((value, earlier))[0]
    exchange = lambda a, axis: lax.all_to_all(a, axis, split_axis=0, concat_axis=0, tiled=True)
    shape = jax.ShapeDtypeStruct

    up_own = jnp.transpose(gate_up_weight[0], (1, 2, 0))
    down_own = down_weight[0]

    sent, by_head, by_token = whole_call(
        state_kernel,
        [
            shape((heads, HEAD + EXTRA, HEAD), BF16),
            shape((heads, tokens), F32),
            shape((tokens, heads), F32),
        ],
        [decay_rate.T, key_rows, value_rows],
        2 * tokens * width * HEAD,
        62,
        [
            pltpu.VMEM((heads, tokens), F32),
            pltpu.VMEM((tokens, width), BF16),
            pltpu.VMEM((tokens, width), BF16),
            pltpu.SemaphoreType.DMA((2, 4)),
            pltpu.SemaphoreType.DMA,
        ],
        (0, 1, 2),
    )
    arrived = exchange(sent, plane)
    (local_out,) = whole_call(
        local_kernel,
        [shape((tokens, width), F32)],
        [queries, key_rows, value_rows, by_head, by_token],
        4 * tokens * width * tokens,
        16,
    )
    within, kept, total = whole_call(
        scan_kernel,
        [
            shape((heads, HEAD, HEAD), F32),
            shape((heads, EXTRA, HEAD), F32),
            shape((HEAD + EXTRA, HEAD), F32),
        ],
        [after(arrived, local_out)],
        2 * heads * HEAD * HEAD,
        8,
    )
    totals = [to_later(total, k) for k in range(1, chips)]
    (carried,) = whole_call(
        carry_kernel,
        [shape((heads, HEAD, HEAD), BF16)],
        [within, kept, *totals],
        2 * heads * HEAD * HEAD,
        8,
    )
    carried_low = exchange(carried, plane)
    index = expert_index.T
    stream, *bins = whole_call(
        stream_kernel,
        [shape((tokens, width), BF16)] + [shape((experts, rows, width), BF16)] * chunks,
        [
            queries,
            local_out,
            gate_logits,
            residual_in,
            carried_low,
            by_token,
            attention_gain[None, :],
            expert_gain[None, :],
            index,
        ],
        2 * tokens * width * (HEAD + chunks * count),
        8,
        [pltpu.VMEM((tokens, width), F32)],
    )

    up_other = swap(after(up_own, stream))
    down_other = swap(after(down_own, stream))
    weights = (up_own, up_other, down_own, down_other)
    wide = lambda a: a.astype(F32)
    plus = lambda *terms: functools.reduce(jnp.add, map(wide, terms)).astype(BF16)

    own_a, own_b = (exchange(bin_rows, "seq").reshape(count, width) for bin_rows in bins)
    left_a, right_a = (go_ahead(own_a), go_back(own_a))
    far_a = go_ahead(left_a)
    right_b = go_back(after(own_b, right_a))
    left_b = go_ahead(after(own_b, far_a))
    far_b = go_back(right_b)
    out_own_a, out_left_a, out_right_a, out_far_a = expert_rows(
        (own_a, left_a, right_a, far_a), *weights
    )
    pass_a, back_a = (go_ahead(out_far_a), go_back(out_left_a))
    out_own_b, out_left_b, out_right_b, out_far_b = expert_rows(
        (own_b, left_b, right_b, far_b), *weights
    )
    pass_b = go_back(after(out_far_b, pass_a, back_a))
    ahead_a = go_ahead(plus(out_right_a, pass_a))
    ahead_b = go_ahead(after(out_right_b, ahead_a))
    to_left_b = plus(out_left_b, pass_b)
    back_b = go_back(to_left_b)
    home = lambda *terms: plus(*terms).reshape(experts, rows, width)
    returned = [
        exchange(after(home(out_own_a, ahead_a, back_a), to_left_b), "seq"),
        exchange(home(out_own_b, ahead_b, back_b), "seq"),
    ]
    (out,) = whole_call(
        mix_kernel,
        [shape((tokens, width), BF16)],
        [stream, index, router_weight.T, *returned],
        4 * tokens * width * count * chunks,
        16,
    )
    return out


def solution(mesh):
    groups, experts = (mesh.shape["grp"], mesh.shape["seq"])
    split = Mesh(mesh.devices.reshape(groups // 2, 2, experts), ("x", "core", "seq"))
    rows = P(("x", "core", "seq"), None)
    return jax.shard_map(
        body,
        mesh=split,
        in_specs=(
            rows,
            rows,
            rows,
            rows,
            rows,
            rows,
            P(),
            P(),
            rows,
            rows,
            P("seq", None, None, ("x", "core")),
            P("seq", ("x", "core"), None),
        ),
        out_specs=rows,
        check_vma=False,
    )
```

```python
import functools

import jax
import jax.numpy as jnp
from jax import lax
from jax.experimental import pallas as pl
from jax.experimental.pallas import tpu as pltpu
from jax.sharding import Mesh
from jax.sharding import PartitionSpec as P

F32, BF16 = (jnp.float32, jnp.bfloat16)
HEAD = 128
EXTRA = 8
MIB = 1 << 20
NT = (((1,), (1,)), ((), ()))
TN = (((0,), (0,)), ((), ()))


def vmem(count):
    return [pl.BlockSpec(memory_space=pltpu.VMEM)] * count


def whole_call(kernel, outs, args, flops, limit, scratch=(), in_place=()):
    moved = sum(a.size * a.dtype.itemsize for a in (*args, *outs))
    return pl.pallas_call(
        kernel,
        out_shape=outs,
        in_specs=[
            pl.BlockSpec(memory_space=pltpu.HBM if place in in_place else pltpu.VMEM)
            for place in range(len(args))
        ],
        out_specs=vmem(len(outs)),
        scratch_shapes=list(scratch),
        cost_estimate=pl.CostEstimate(flops=flops, bytes_accessed=moved, transcendentals=0),
        compiler_params=pltpu.CompilerParams(vmem_limit_bytes=limit * MIB),
    )(*args)


def lane_block(h):
    return slice(h * HEAD, (h + 1) * HEAD)


def state_kernel(
    rates_in_ref,
    key_rows_ref,
    value_rows_ref,
    sent_ref,
    by_head_ref,
    by_token_ref,
    rates_ref,
    key_ref,
    value_ref,
    loaded,
    rates_loaded,
):
    heads, tokens = rates_ref.shape
    rates_copy = pltpu.make_async_copy(rates_in_ref, rates_ref, rates_loaded)
    rates_copy.start()
    groups = loaded.shape[1]
    columns = heads * HEAD // groups
    copies = [
        [
            pltpu.make_async_copy(
                source.at[:, pl.ds(g * columns, columns)],
                target.at[:, pl.ds(g * columns, columns)],
                loaded.at[place, g],
            )
            for place, (source, target) in enumerate(
                ((key_rows_ref, key_ref), (value_rows_ref, value_ref))
            )
        ]
        for g in range(groups)
    ]
    for pair in copies:
        for copy in pair:
            copy.start()
    rates_copy.wait()
    at = lambda dim: lax.broadcasted_iota(jnp.int32, (tokens, tokens), dim)
    upto = (at(0) <= at(1)).astype(F32)
    by_head = jnp.dot(
        rates_ref[...], upto, precision=lax.Precision.HIGHEST, preferred_element_type=F32
    )
    by_token = by_head.T
    by_head_ref[...] = by_head
    by_token_ref[...] = by_token
    fade = jnp.exp(by_token - by_token[tokens - 1 :, :])
    keep = jnp.broadcast_to(jnp.exp(-by_head[:, tokens - 1 :]), (heads, HEAD))
    high = keep.astype(BF16).astype(F32)
    middle = (keep - high).astype(BF16).astype(F32)
    low = keep - high - middle
    row = lax.broadcasted_iota(jnp.int32, (EXTRA, HEAD), 0)
    for h in range(heads):
        if h % (heads // groups) == 0:
            for copy in copies[h // (heads // groups)]:
                copy.wait()
        faded = (key_ref[:, lane_block(h)].astype(F32) * fade[:, h : h + 1]).astype(BF16)
        state = lax.dot_general(faded, value_ref[:, lane_block(h)], TN, preferred_element_type=F32)
        tail = jnp.where(row == 0, high[h : h + 1], 0.0)
        tail = jnp.where(row == 1, middle[h : h + 1], tail)
        tail = jnp.where(row == 2, low[h : h + 1], tail).astype(BF16)
        sent_ref[h, :HEAD, :] = state.astype(BF16)
        sent_ref[h, HEAD:, :] = tail


def scan_kernel(arrived_ref, within_ref, kept_ref, total_ref):
    def step(block, carry):
        state, kept = carry
        within_ref[block] = state
        kept_ref[block] = kept
        tail = arrived_ref[block, HEAD:, :].astype(F32)
        keep = tail[0:1] + tail[1:2] + tail[2:3]
        return keep * state + arrived_ref[block, :HEAD, :].astype(F32), keep * kept

    start = (jnp.zeros((HEAD, HEAD), F32), jnp.ones((EXTRA, HEAD), F32))
    state, kept = lax.fori_loop(0, within_ref.shape[0], step, start, unroll=4)
    total_ref[:HEAD, :] = state
    total_ref[HEAD:, :] = kept


def carry_kernel(within_ref, kept_ref, *rest):
    *total_refs, carried_ref = rest
    before = jnp.zeros((HEAD, HEAD), F32)
    for total_ref in reversed(total_refs):
        before = total_ref[:HEAD, :] + total_ref[HEAD : HEAD + 1, :] * before

    def step(block, _):
        carried = within_ref[block] + kept_ref[block, 0:1, :] * before
        carried_ref[block] = carried.astype(BF16)
        return 0

    lax.fori_loop(0, carried_ref.shape[0], step, 0, unroll=4)


def local_kernel(
    query_ref,
    key_ref,
    value_ref,
    by_head_ref,
    by_token_ref,
    out_ref,
):
    heads, tokens = by_head_ref.shape
    at = lambda dim: lax.broadcasted_iota(jnp.int32, (tokens, tokens), dim)
    causal = at(0) >= at(1)
    for h in range(heads):
        scores = lax.dot_general(
            query_ref[:, lane_block(h)], key_ref[:, lane_block(h)], NT, preferred_element_type=F32
        )
        spacing = by_head_ref[h : h + 1, :] - by_token_ref[:, h : h + 1]
        fading = jnp.exp(jnp.minimum(spacing, 0.0))
        weights = jnp.where(causal, scores * fading, 0.0).astype(BF16)
        out_ref[:, lane_block(h)] = jnp.dot(
            weights, value_ref[:, lane_block(h)], preferred_element_type=F32
        )


def places(index_ref, experts):
    tokens = index_ref.shape[1]
    expert = lax.broadcasted_iota(jnp.int32, (experts, tokens), 0)
    first, second = (index_ref[0:1, :] == expert, index_ref[1:2, :] == expert)
    named = (first | second).astype(F32)
    at = lambda dim: lax.broadcasted_iota(jnp.int32, (tokens, tokens), dim)
    earlier = (at(0) < at(1)).astype(BF16)
    slot = jnp.dot(named.astype(BF16), earlier, preferred_element_type=F32)
    return first, second, jnp.where(named > 0.0, slot, -1.0)


def chunk_rows(slot, chunk, rows):
    experts, tokens = slot.shape
    wanted = lax.broadcasted_iota(jnp.int32, (rows, tokens), 0).astype(F32) + float(chunk * rows)
    return [slot[e : e + 1, :] == wanted for e in range(experts)]


def stream_kernel(
    query_ref,
    local_ref,
    gate_ref,
    residual_ref,
    carried_ref,
    by_token_ref,
    attention_gain_ref,
    expert_gain_ref,
    index_ref,
    stream_ref,
    *rest,
):
    *bin_refs, attention_ref = rest
    tokens, width = query_ref.shape
    heads = width // HEAD
    since = jnp.exp(-by_token_ref[...])
    total = jnp.zeros((tokens, HEAD), F32)
    for h in range(heads):
        carried_out = jnp.dot(
            query_ref[:, lane_block(h)], carried_ref[h], preferred_element_type=F32
        )
        attention = local_ref[:, lane_block(h)] + since[:, h : h + 1] * carried_out
        attention_ref[:, lane_block(h)] = attention
        total = total + attention * attention
    inverse = lax.rsqrt(jnp.sum(total, axis=1, keepdims=True) / width + 1e-05)
    total = jnp.zeros((tokens, HEAD), F32)
    for h in range(heads):
        gate = gate_ref[:, lane_block(h)].astype(F32)
        gain = attention_gain_ref[:, lane_block(h)] / (1.0 + jnp.exp(-gate))
        gated = attention_ref[:, lane_block(h)] * inverse * gain
        stream = (residual_ref[:, lane_block(h)].astype(F32) + gated).astype(BF16)
        stream_ref[:, lane_block(h)] = stream
        wide = stream.astype(F32)
        total = total + wide * wide
    inverse = lax.rsqrt(jnp.sum(total, axis=1, keepdims=True) / width + 1e-05)
    experts = bin_refs[0].shape[0]
    rows = bin_refs[0].shape[1]
    slot = places(index_ref, experts)[2]
    selectors = [
        jnp.concatenate([m.astype(F32) for m in chunk_rows(slot, c, rows)], axis=0).astype(BF16)
        for c in range(len(bin_refs))
    ]
    for h in range(heads):
        wide = stream_ref[:, lane_block(h)].astype(F32)
        entry = (wide * inverse * expert_gain_ref[:, lane_block(h)]).astype(BF16)
        for selector, bin_ref in zip(selectors, bin_refs):
            picked = jnp.dot(selector, entry, preferred_element_type=F32)
            bin_ref[:, :, lane_block(h)] = picked.astype(BF16).reshape(experts, rows, HEAD)


def mix_kernel(stream_ref, index_ref, router_ref, *rest):
    *returned_refs, out_ref = rest
    experts, rows, width = returned_refs[0].shape
    first, second, slot = places(index_ref, experts)
    scale = jnp.where(first, router_ref[0:1, :], 0.0) + jnp.where(second, router_ref[1:2, :], 0.0)
    weights = []
    for c in range(len(returned_refs)):
        masks = chunk_rows(slot, c, rows)
        chosen = jnp.concatenate(
            [jnp.where(m, scale[e : e + 1, :], 0.0) for e, m in enumerate(masks)], axis=0
        ).T
        high = chosen.astype(BF16)
        weights.append((high, (chosen - high.astype(F32)).astype(BF16)))
    for h in range(width // HEAD // 4):
        columns = slice(h * 4 * HEAD, (h + 1) * 4 * HEAD)
        total = stream_ref[:, columns].astype(F32)
        for (high, low), returned_ref in zip(weights, returned_refs):
            returned = returned_ref[:, :, columns].reshape(experts * rows, 4 * HEAD)
            total = total + jnp.dot(high, returned, preferred_element_type=F32)
            total = total + jnp.dot(low, returned, preferred_element_type=F32)
        out_ref[:, columns] = total.astype(BF16)


def expert_kernel(
    own_ref,
    left_ref,
    right_ref,
    far_ref,
    up_own_ref,
    up_other_ref,
    down_own_ref,
    down_other_ref,
    out_own_ref,
    out_left_ref,
    out_right_ref,
    out_far_ref,
    rows_ref,
    up_ref,
    down_ref,
    turned_ref,
    hidden_ref,
    up_sem,
    down_sem,
):
    count = own_ref.shape[0]
    tiles, _, tile, width = up_ref.shape
    units = down_own_ref.shape[0]
    parts, _, columns = down_ref.shape
    each = tiles // 2

    def up_copies(k):
        source = (up_own_ref, up_other_ref)[k // each]
        part = source.at[:, pl.ds(k % each * tile, tile), :]
        return [pltpu.make_async_copy(part, up_ref.at[k], up_sem.at[k])]

    def down_copies(k):
        return [
            pltpu.make_async_copy(
                source.at[:, pl.ds(k * columns, columns)],
                down_ref.at[k, pl.ds(place * units, units), :],
                down_sem.at[k, place],
            )
            for place, source in enumerate((down_own_ref, down_other_ref))
        ]

    loads = [up_copies(k) for k in range(tiles)] + [down_copies(k) for k in range(parts)]
    in_flight = 2

    def start(k):
        if k < len(loads):
            for copy in loads[k]:
                copy.start()

    def arrive(k):
        for copy in loads[k]:
            copy.wait()
        start(k + in_flight)

    for k in range(in_flight):
        start(k)
    rows_ref[0:count] = own_ref[...]
    rows_ref[count : 2 * count] = left_ref[...]
    rows_ref[2 * count : 3 * count] = right_ref[...]
    rows_ref[3 * count :] = far_ref[...]
    for k in range(tiles):
        arrive(k)
        both = up_ref[k].reshape(2 * tile, width)
        pair = lax.dot_general(both, rows_ref[...], NT, preferred_element_type=F32)
        gate, up = (pair[:tile], pair[tile:])
        hidden = gate / (1.0 + jnp.exp(-gate)) * up
        turned_ref[k * tile : (k + 1) * tile, :] = hidden.astype(BF16)
    hidden_ref[...] = turned_ref[...].T
    for k in range(parts):
        arrive(tiles + k)
        out = jnp.dot(hidden_ref[...], down_ref[k], preferred_element_type=F32).astype(BF16)
        for place, ref in enumerate((out_own_ref, out_left_ref, out_right_ref, out_far_ref)):
            ref[:, k * columns : (k + 1) * columns] = out[place * count : (place + 1) * count]


def expert_rows(blocks, up_own, up_other, down_own, down_other):
    count, width = blocks[0].shape
    units = down_own.shape[0]
    tiles, parts = (4, 4)
    tile, columns = (2 * units // tiles, width // parts)
    in_place = [pl.BlockSpec(memory_space=pltpu.HBM)] * 4
    return pl.pallas_call(
        expert_kernel,
        in_specs=vmem(len(blocks)) + in_place,
        out_specs=vmem(4),
        out_shape=[jax.ShapeDtypeStruct((count, width), BF16)] * 4,
        scratch_shapes=[
            pltpu.VMEM((4 * count, width), BF16),
            pltpu.VMEM((tiles, 2, tile, width), BF16),
            pltpu.VMEM((parts, 2 * units, columns), BF16),
            pltpu.VMEM((2 * units, 4 * count), BF16),
            pltpu.VMEM((4 * count, 2 * units), BF16),
            pltpu.SemaphoreType.DMA((tiles,)),
            pltpu.SemaphoreType.DMA((parts, 2)),
        ],
        cost_estimate=pl.CostEstimate(
            flops=4 * count * 2 * units * width * 6,
            bytes_accessed=6 * units * width * 2 + 8 * count * width * 2,
            transcendentals=0,
        ),
        compiler_params=pltpu.CompilerParams(vmem_limit_bytes=46 * MIB),
    )(*blocks, up_own, up_other, down_own, down_other)


def body(
    queries,
    key_rows,
    value_rows,
    gate_logits,
    residual_in,
    decay_rate,
    attention_gain,
    expert_gain,
    expert_index,
    router_weight,
    gate_up_weight,
    down_weight,
):
    chips, experts = (lax.axis_size("x"), lax.axis_size("seq"))
    tokens, width = queries.shape
    heads = decay_rate.shape[1]
    chunks = 2
    slots = tokens * expert_index.shape[1] // experts
    rows = slots // chunks
    count = experts * rows

    swap = lambda a: lax.ppermute(a, "core", [(0, 1), (1, 0)])
    go_ahead = lambda a: lax.ppermute(a, "x", [(i, (i + 1) % chips) for i in range(chips)])
    go_back = lambda a: lax.ppermute(a, "x", [(i, (i - 1) % chips) for i in range(chips)])
    to_later = lambda a, k: lax.ppermute(a, "x", [(i, i + k) for i in range(chips - k)])
    plane = ("core", "seq")
    after = lambda value, *earlier: lax.optimization_barrier((value, earlier))[0]
    exchange = lambda a, axis: lax.all_to_all(a, axis, split_axis=0, concat_axis=0, tiled=True)
    shape = jax.ShapeDtypeStruct

    up_own = jnp.transpose(gate_up_weight[0], (1, 2, 0))
    down_own = down_weight[0]

    sent, by_head, by_token = whole_call(
        state_kernel,
        [
            shape((heads, HEAD + EXTRA, HEAD), BF16),
            shape((heads, tokens), F32),
            shape((tokens, heads), F32),
        ],
        [decay_rate.T, key_rows, value_rows],
        2 * tokens * width * HEAD,
        62,
        [
            pltpu.VMEM((heads, tokens), F32),
            pltpu.VMEM((tokens, width), BF16),
            pltpu.VMEM((tokens, width), BF16),
            pltpu.SemaphoreType.DMA((2, 4)),
            pltpu.SemaphoreType.DMA,
        ],
        (0, 1, 2),
    )
    arrived = exchange(sent, plane)
    (local_out,) = whole_call(
        local_kernel,
        [shape((tokens, width), F32)],
        [queries, key_rows, value_rows, by_head, by_token],
        4 * tokens * width * tokens,
        16,
    )
    within, kept, total = whole_call(
        scan_kernel,
        [
            shape((heads, HEAD, HEAD), F32),
            shape((heads, EXTRA, HEAD), F32),
            shape((HEAD + EXTRA, HEAD), F32),
        ],
        [after(arrived, local_out)],
        2 * heads * HEAD * HEAD,
        8,
    )
    totals = [to_later(total, k) for k in range(chips - 1, 0, -1)][::-1]
    (carried,) = whole_call(
        carry_kernel,
        [shape((heads, HEAD, HEAD), BF16)],
        [within, kept, *totals],
        2 * heads * HEAD * HEAD,
        8,
    )
    carried_low = exchange(carried, plane)
    index = expert_index.T
    stream, *bins = whole_call(
        stream_kernel,
        [shape((tokens, width), BF16)] + [shape((experts, rows, width), BF16)] * chunks,
        [
            queries,
            local_out,
            gate_logits,
            residual_in,
            carried_low,
            by_token,
            attention_gain[None, :],
            expert_gain[None, :],
            index,
        ],
        2 * tokens * width * (HEAD + chunks * count),
        8,
        [pltpu.VMEM((tokens, width), F32)],
    )

    up_other = swap(after(up_own, stream))
    down_other = swap(after(down_own, stream))
    weights = (up_own, up_other, down_own, down_other)
    wide = lambda a: a.astype(F32)
    plus = lambda *terms: functools.reduce(jnp.add, map(wide, terms)).astype(BF16)

    own_a, own_b = (exchange(bin_rows, "seq").reshape(count, width) for bin_rows in bins)
    left_a, right_a = (go_ahead(own_a), go_back(own_a))
    far_a = go_ahead(left_a)
    right_b = go_back(after(own_b, right_a))
    left_b = go_ahead(after(own_b, far_a))
    far_b = go_back(right_b)
    out_own_a, out_left_a, out_right_a, out_far_a = expert_rows(
        (own_a, left_a, right_a, far_a), *weights
    )
    pass_a, back_a = (go_ahead(out_far_a), go_back(out_left_a))
    out_own_b, out_left_b, out_right_b, out_far_b = expert_rows(
        (own_b, left_b, right_b, far_b), *weights
    )
    pass_b = go_back(after(out_far_b, pass_a, back_a))
    ahead_a = go_ahead(plus(out_right_a, pass_a))
    ahead_b = go_ahead(after(out_right_b, ahead_a))
    to_left_b = plus(out_left_b, pass_b)
    back_b = go_back(to_left_b)
    home = lambda *terms: plus(*terms).reshape(experts, rows, width)
    returned_a = exchange(after(home(out_own_a, ahead_a, back_a), to_left_b), "seq")
    returned_b = exchange(home(after(out_own_b, returned_a), ahead_b, back_b), "seq")
    (out,) = whole_call(
        mix_kernel,
        [shape((tokens, width), BF16)],
        [stream, index, router_weight.T, returned_a, returned_b],
        4 * tokens * width * count * chunks,
        16,
    )
    return out


def solution(mesh):
    groups, experts = (mesh.shape["grp"], mesh.shape["seq"])
    split = Mesh(mesh.devices.reshape(groups // 2, 2, experts), ("x", "core", "seq"))
    rows = P(("x", "core", "seq"), None)
    return jax.shard_map(
        body,
        mesh=split,
        in_specs=(
            rows,
            rows,
            rows,
            rows,
            rows,
            rows,
            P(),
            P(),
            rows,
            rows,
            P("seq", None, None, ("x", "core")),
            P("seq", ("x", "core"), None),
        ),
        out_specs=rows,
        check_vma=False,
    )
```

```python
import functools

import jax
import jax.numpy as jnp
from jax import lax
from jax.experimental import pallas as pl
from jax.experimental.pallas import tpu as pltpu
from jax.sharding import Mesh
from jax.sharding import PartitionSpec as P

F32, BF16 = (jnp.float32, jnp.bfloat16)
HEAD = 128
EXTRA = 8
MIB = 1 << 20
NT = (((1,), (1,)), ((), ()))
TN = (((0,), (0,)), ((), ()))


def vmem(count):
    return [pl.BlockSpec(memory_space=pltpu.VMEM)] * count


def whole_call(kernel, outs, args, flops, limit, scratch=(), in_place=()):
    moved = sum(a.size * a.dtype.itemsize for a in (*args, *outs))
    return pl.pallas_call(
        kernel,
        out_shape=outs,
        in_specs=[
            pl.BlockSpec(memory_space=pltpu.HBM if place in in_place else pltpu.VMEM)
            for place in range(len(args))
        ],
        out_specs=vmem(len(outs)),
        scratch_shapes=list(scratch),
        cost_estimate=pl.CostEstimate(flops=flops, bytes_accessed=moved, transcendentals=0),
        compiler_params=pltpu.CompilerParams(vmem_limit_bytes=limit * MIB),
    )(*args)


def lane_block(h):
    return slice(h * HEAD, (h + 1) * HEAD)


def state_kernel(
    rates_in_ref,
    key_rows_ref,
    value_rows_ref,
    sent_ref,
    by_head_ref,
    by_token_ref,
    rates_ref,
    key_ref,
    value_ref,
    loaded,
    rates_loaded,
):
    heads, tokens = rates_ref.shape
    rates_copy = pltpu.make_async_copy(rates_in_ref, rates_ref, rates_loaded)
    rates_copy.start()
    groups = loaded.shape[1]
    columns = heads * HEAD // groups
    copies = [
        [
            pltpu.make_async_copy(
                source.at[:, pl.ds(g * columns, columns)],
                target.at[:, pl.ds(g * columns, columns)],
                loaded.at[place, g],
            )
            for place, (source, target) in enumerate(
                ((key_rows_ref, key_ref), (value_rows_ref, value_ref))
            )
        ]
        for g in range(groups)
    ]
    for pair in copies:
        for copy in pair:
            copy.start()
    rates_copy.wait()
    at = lambda dim: lax.broadcasted_iota(jnp.int32, (tokens, tokens), dim)
    upto = (at(0) <= at(1)).astype(F32)
    by_head = jnp.dot(
        rates_ref[...], upto, precision=lax.Precision.HIGHEST, preferred_element_type=F32
    )
    by_token = by_head.T
    by_head_ref[...] = by_head
    by_token_ref[...] = by_token
    fade = jnp.exp(by_token - by_token[tokens - 1 :, :])
    keep = jnp.broadcast_to(jnp.exp(-by_head[:, tokens - 1 :]), (heads, HEAD))
    high = keep.astype(BF16).astype(F32)
    middle = (keep - high).astype(BF16).astype(F32)
    low = keep - high - middle
    row = lax.broadcasted_iota(jnp.int32, (EXTRA, HEAD), 0)
    for h in range(heads):
        if h % (heads // groups) == 0:
            for copy in copies[h // (heads // groups)]:
                copy.wait()
        faded = (key_ref[:, lane_block(h)].astype(F32) * fade[:, h : h + 1]).astype(BF16)
        state = lax.dot_general(faded, value_ref[:, lane_block(h)], TN, preferred_element_type=F32)
        tail = jnp.where(row == 0, high[h : h + 1], 0.0)
        tail = jnp.where(row == 1, middle[h : h + 1], tail)
        tail = jnp.where(row == 2, low[h : h + 1], tail).astype(BF16)
        sent_ref[h, :HEAD, :] = state.astype(BF16)
        sent_ref[h, HEAD:, :] = tail


def scan_kernel(arrived_ref, within_ref, kept_ref, total_ref):
    def step(block, carry):
        state, kept = carry
        within_ref[block] = state
        kept_ref[block] = kept
        tail = arrived_ref[block, HEAD:, :].astype(F32)
        keep = tail[0:1] + tail[1:2] + tail[2:3]
        return keep * state + arrived_ref[block, :HEAD, :].astype(F32), keep * kept

    start = (jnp.zeros((HEAD, HEAD), F32), jnp.ones((EXTRA, HEAD), F32))
    state, kept = lax.fori_loop(0, within_ref.shape[0], step, start, unroll=4)
    total_ref[:HEAD, :] = state
    total_ref[HEAD:, :] = kept


def carry_kernel(within_ref, kept_ref, earlier_ref, *rest):
    *total_refs, carried_ref = rest
    before = jnp.zeros((HEAD, HEAD), F32)
    for place, total_ref in reversed(list(enumerate(total_refs))):
        longer = total_ref[:HEAD, :] + total_ref[HEAD : HEAD + 1, :] * before
        before = jnp.where(earlier_ref[place : place + 1, :] > 0.0, longer, before)

    def step(block, _):
        carried = within_ref[block] + kept_ref[block, 0:1, :] * before
        carried_ref[block] = carried.astype(BF16)
        return 0

    lax.fori_loop(0, carried_ref.shape[0], step, 0, unroll=4)


def local_kernel(
    query_ref,
    key_ref,
    value_ref,
    by_head_ref,
    by_token_ref,
    out_ref,
):
    heads, tokens = by_head_ref.shape
    at = lambda dim: lax.broadcasted_iota(jnp.int32, (tokens, tokens), dim)
    causal = at(0) >= at(1)
    for h in range(heads):
        scores = lax.dot_general(
            query_ref[:, lane_block(h)], key_ref[:, lane_block(h)], NT, preferred_element_type=F32
        )
        spacing = by_head_ref[h : h + 1, :] - by_token_ref[:, h : h + 1]
        fading = jnp.exp(jnp.minimum(spacing, 0.0))
        weights = jnp.where(causal, scores * fading, 0.0).astype(BF16)
        out_ref[:, lane_block(h)] = jnp.dot(
            weights, value_ref[:, lane_block(h)], preferred_element_type=F32
        )


def places(index_ref, experts):
    tokens = index_ref.shape[1]
    expert = lax.broadcasted_iota(jnp.int32, (experts, tokens), 0)
    first, second = (index_ref[0:1, :] == expert, index_ref[1:2, :] == expert)
    named = (first | second).astype(F32)
    at = lambda dim: lax.broadcasted_iota(jnp.int32, (tokens, tokens), dim)
    earlier = (at(0) < at(1)).astype(BF16)
    slot = jnp.dot(named.astype(BF16), earlier, preferred_element_type=F32)
    return first, second, jnp.where(named > 0.0, slot, -1.0)


def chunk_rows(slot, chunk, rows):
    experts, tokens = slot.shape
    wanted = lax.broadcasted_iota(jnp.int32, (rows, tokens), 0).astype(F32) + float(chunk * rows)
    return [slot[e : e + 1, :] == wanted for e in range(experts)]


def stream_kernel(
    query_ref,
    local_ref,
    gate_ref,
    residual_ref,
    carried_ref,
    by_token_ref,
    attention_gain_ref,
    expert_gain_ref,
    index_ref,
    stream_ref,
    *rest,
):
    *bin_refs, attention_ref = rest
    tokens, width = query_ref.shape
    heads = width // HEAD
    since = jnp.exp(-by_token_ref[...])
    total = jnp.zeros((tokens, HEAD), F32)
    for h in range(heads):
        carried_out = jnp.dot(
            query_ref[:, lane_block(h)], carried_ref[h], preferred_element_type=F32
        )
        attention = local_ref[:, lane_block(h)] + since[:, h : h + 1] * carried_out
        attention_ref[:, lane_block(h)] = attention
        total = total + attention * attention
    inverse = lax.rsqrt(jnp.sum(total, axis=1, keepdims=True) / width + 1e-05)
    total = jnp.zeros((tokens, HEAD), F32)
    for h in range(heads):
        gate = gate_ref[:, lane_block(h)].astype(F32)
        gain = attention_gain_ref[:, lane_block(h)] / (1.0 + jnp.exp(-gate))
        gated = attention_ref[:, lane_block(h)] * inverse * gain
        stream = (residual_ref[:, lane_block(h)].astype(F32) + gated).astype(BF16)
        stream_ref[:, lane_block(h)] = stream
        wide = stream.astype(F32)
        total = total + wide * wide
    inverse = lax.rsqrt(jnp.sum(total, axis=1, keepdims=True) / width + 1e-05)
    experts = bin_refs[0].shape[0]
    rows = bin_refs[0].shape[1]
    slot = places(index_ref, experts)[2]
    selectors = [
        jnp.concatenate([m.astype(F32) for m in chunk_rows(slot, c, rows)], axis=0).astype(BF16)
        for c in range(len(bin_refs))
    ]
    for h in range(heads):
        wide = stream_ref[:, lane_block(h)].astype(F32)
        entry = (wide * inverse * expert_gain_ref[:, lane_block(h)]).astype(BF16)
        for selector, bin_ref in zip(selectors, bin_refs):
            picked = jnp.dot(selector, entry, preferred_element_type=F32)
            bin_ref[:, :, lane_block(h)] = picked.astype(BF16).reshape(experts, rows, HEAD)


def mix_kernel(stream_ref, index_ref, router_ref, *rest):
    *returned_refs, out_ref = rest
    experts, rows, width = returned_refs[0].shape
    first, second, slot = places(index_ref, experts)
    scale = jnp.where(first, router_ref[0:1, :], 0.0) + jnp.where(second, router_ref[1:2, :], 0.0)
    weights = []
    for c in range(len(returned_refs)):
        masks = chunk_rows(slot, c, rows)
        chosen = jnp.concatenate(
            [jnp.where(m, scale[e : e + 1, :], 0.0) for e, m in enumerate(masks)], axis=0
        ).T
        high = chosen.astype(BF16)
        weights.append((high, (chosen - high.astype(F32)).astype(BF16)))
    for h in range(width // HEAD // 4):
        columns = slice(h * 4 * HEAD, (h + 1) * 4 * HEAD)
        total = stream_ref[:, columns].astype(F32)
        for (high, low), returned_ref in zip(weights, returned_refs):
            returned = returned_ref[:, :, columns].reshape(experts * rows, 4 * HEAD)
            total = total + jnp.dot(high, returned, preferred_element_type=F32)
            total = total + jnp.dot(low, returned, preferred_element_type=F32)
        out_ref[:, columns] = total.astype(BF16)


def expert_kernel(
    own_ref,
    left_ref,
    right_ref,
    far_ref,
    up_own_ref,
    up_other_ref,
    down_own_ref,
    down_other_ref,
    out_own_ref,
    out_left_ref,
    out_right_ref,
    out_far_ref,
    rows_ref,
    up_ref,
    down_ref,
    turned_ref,
    hidden_ref,
    up_sem,
    down_sem,
):
    count = own_ref.shape[0]
    tiles, _, tile, width = up_ref.shape
    units = down_own_ref.shape[0]
    parts, _, columns = down_ref.shape
    each = tiles // 2

    def up_copies(k):
        source = (up_own_ref, up_other_ref)[k // each]
        part = source.at[:, pl.ds(k % each * tile, tile), :]
        return [pltpu.make_async_copy(part, up_ref.at[k], up_sem.at[k])]

    def down_copies(k):
        return [
            pltpu.make_async_copy(
                source.at[:, pl.ds(k * columns, columns)],
                down_ref.at[k, pl.ds(place * units, units), :],
                down_sem.at[k, place],
            )
            for place, source in enumerate((down_own_ref, down_other_ref))
        ]

    loads = [up_copies(k) for k in range(tiles)] + [down_copies(k) for k in range(parts)]
    in_flight = 2

    def start(k):
        if k < len(loads):
            for copy in loads[k]:
                copy.start()

    def arrive(k):
        for copy in loads[k]:
            copy.wait()
        start(k + in_flight)

    for k in range(in_flight):
        start(k)
    rows_ref[0:count] = own_ref[...]
    rows_ref[count : 2 * count] = left_ref[...]
    rows_ref[2 * count : 3 * count] = right_ref[...]
    rows_ref[3 * count :] = far_ref[...]
    for k in range(tiles):
        arrive(k)
        both = up_ref[k].reshape(2 * tile, width)
        pair = lax.dot_general(both, rows_ref[...], NT, preferred_element_type=F32)
        gate, up = (pair[:tile], pair[tile:])
        hidden = gate / (1.0 + jnp.exp(-gate)) * up
        turned_ref[k * tile : (k + 1) * tile, :] = hidden.astype(BF16)
    hidden_ref[...] = turned_ref[...].T
    for k in range(parts):
        arrive(tiles + k)
        out = jnp.dot(hidden_ref[...], down_ref[k], preferred_element_type=F32).astype(BF16)
        for place, ref in enumerate((out_own_ref, out_left_ref, out_right_ref, out_far_ref)):
            ref[:, k * columns : (k + 1) * columns] = out[place * count : (place + 1) * count]


def expert_rows(blocks, up_own, up_other, down_own, down_other):
    count, width = blocks[0].shape
    units = down_own.shape[0]
    tiles, parts = (4, 4)
    tile, columns = (2 * units // tiles, width // parts)
    in_place = [pl.BlockSpec(memory_space=pltpu.HBM)] * 4
    return pl.pallas_call(
        expert_kernel,
        in_specs=vmem(len(blocks)) + in_place,
        out_specs=vmem(4),
        out_shape=[jax.ShapeDtypeStruct((count, width), BF16)] * 4,
        scratch_shapes=[
            pltpu.VMEM((4 * count, width), BF16),
            pltpu.VMEM((tiles, 2, tile, width), BF16),
            pltpu.VMEM((parts, 2 * units, columns), BF16),
            pltpu.VMEM((2 * units, 4 * count), BF16),
            pltpu.VMEM((4 * count, 2 * units), BF16),
            pltpu.SemaphoreType.DMA((tiles,)),
            pltpu.SemaphoreType.DMA((parts, 2)),
        ],
        cost_estimate=pl.CostEstimate(
            flops=4 * count * 2 * units * width * 6,
            bytes_accessed=6 * units * width * 2 + 8 * count * width * 2,
            transcendentals=0,
        ),
        compiler_params=pltpu.CompilerParams(vmem_limit_bytes=46 * MIB),
    )(*blocks, up_own, up_other, down_own, down_other)


def body(
    queries,
    key_rows,
    value_rows,
    gate_logits,
    residual_in,
    decay_rate,
    attention_gain,
    expert_gain,
    expert_index,
    router_weight,
    gate_up_weight,
    down_weight,
):
    chips, experts = (lax.axis_size("x"), lax.axis_size("seq"))
    tokens, width = queries.shape
    heads = decay_rate.shape[1]
    chunks = 2
    slots = tokens * expert_index.shape[1] // experts
    rows = slots // chunks
    count = experts * rows

    swap = lambda a: lax.ppermute(a, "core", [(0, 1), (1, 0)])
    go_ahead = lambda a: lax.ppermute(a, "x", [(i, (i + 1) % chips) for i in range(chips)])
    go_back = lambda a: lax.ppermute(a, "x", [(i, (i - 1) % chips) for i in range(chips)])
    to_later = lambda a, k: lax.ppermute(a, "x", [(i, (i + k) % chips) for i in range(chips)])
    plane = ("core", "seq")
    after = lambda value, *earlier: lax.optimization_barrier((value, earlier))[0]
    exchange = lambda a, axis: lax.all_to_all(a, axis, split_axis=0, concat_axis=0, tiled=True)
    shape = jax.ShapeDtypeStruct

    up_own = jnp.transpose(gate_up_weight[0], (1, 2, 0))
    down_own = down_weight[0]

    sent, by_head, by_token = whole_call(
        state_kernel,
        [
            shape((heads, HEAD + EXTRA, HEAD), BF16),
            shape((heads, tokens), F32),
            shape((tokens, heads), F32),
        ],
        [decay_rate.T, key_rows, value_rows],
        2 * tokens * width * HEAD,
        62,
        [
            pltpu.VMEM((heads, tokens), F32),
            pltpu.VMEM((tokens, width), BF16),
            pltpu.VMEM((tokens, width), BF16),
            pltpu.SemaphoreType.DMA((2, 4)),
            pltpu.SemaphoreType.DMA,
        ],
        (0, 1, 2),
    )
    arrived = exchange(sent, plane)
    (local_out,) = whole_call(
        local_kernel,
        [shape((tokens, width), F32)],
        [queries, key_rows, value_rows, by_head, by_token],
        4 * tokens * width * tokens,
        16,
    )
    within, kept, total = whole_call(
        scan_kernel,
        [
            shape((heads, HEAD, HEAD), F32),
            shape((heads, EXTRA, HEAD), F32),
            shape((HEAD + EXTRA, HEAD), F32),
        ],
        [after(arrived, local_out)],
        2 * heads * HEAD * HEAD,
        8,
    )
    distance = lax.broadcasted_iota(jnp.int32, (chips - 1, HEAD), 0) + 1
    earlier = (distance <= lax.axis_index("x")).astype(F32)
    totals = [to_later(total, k) for k in range(1, chips)]
    (carried,) = whole_call(
        carry_kernel,
        [shape((heads, HEAD, HEAD), BF16)],
        [within, kept, earlier, *totals],
        2 * heads * HEAD * HEAD,
        8,
    )
    carried_low = exchange(carried, plane)
    index = expert_index.T
    stream, *bins = whole_call(
        stream_kernel,
        [shape((tokens, width), BF16)] + [shape((experts, rows, width), BF16)] * chunks,
        [
            queries,
            local_out,
            gate_logits,
            residual_in,
            carried_low,
            by_token,
            attention_gain[None, :],
            expert_gain[None, :],
            index,
        ],
        2 * tokens * width * (HEAD + chunks * count),
        8,
        [pltpu.VMEM((tokens, width), F32)],
    )

    up_other = swap(after(up_own, stream))
    down_other = swap(after(down_own, stream))
    weights = (up_own, up_other, down_own, down_other)
    wide = lambda a: a.astype(F32)
    plus = lambda *terms: functools.reduce(jnp.add, map(wide, terms)).astype(BF16)

    own_a, own_b = (exchange(bin_rows, "seq").reshape(count, width) for bin_rows in bins)
    left_a, right_a = (go_ahead(own_a), go_back(own_a))
    far_a = go_ahead(after(left_a, own_b))
    right_b = go_back(after(own_b, right_a, down_other))
    left_b = go_ahead(after(own_b, far_a))
    far_b = go_back(right_b)
    out_own_a, out_left_a, out_right_a, out_far_a = expert_rows(
        (own_a, left_a, right_a, far_a), *weights
    )
    pass_a, back_a = (go_ahead(out_far_a), go_back(out_left_a))
    out_own_b, out_left_b, out_right_b, out_far_b = expert_rows(
        (own_b, left_b, right_b, far_b), *weights
    )
    pass_b = go_back(after(out_far_b, pass_a, back_a))
    ahead_a = go_ahead(plus(out_right_a, pass_a))
    ahead_b = go_ahead(after(out_right_b, ahead_a))
    to_left_b = plus(out_left_b, pass_b)
    back_b = go_back(to_left_b)
    home = lambda *terms: plus(*terms).reshape(experts, rows, width)
    returned_a = exchange(after(home(out_own_a, ahead_a, back_a), to_left_b), "seq")
    returned_b = exchange(home(after(out_own_b, returned_a), ahead_b, back_b), "seq")
    (out,) = whole_call(
        mix_kernel,
        [shape((tokens, width), BF16)],
        [stream, index, router_weight.T, returned_a, returned_b],
        4 * tokens * width * count * chunks,
        16,
    )
    return out


def solution(mesh):
    groups, experts = (mesh.shape["grp"], mesh.shape["seq"])
    split = Mesh(mesh.devices.reshape(groups // 2, 2, experts), ("x", "core", "seq"))
    rows = P(("x", "core", "seq"), None)
    return jax.shard_map(
        body,
        mesh=split,
        in_specs=(
            rows,
            rows,
            rows,
            rows,
            rows,
            rows,
            P(),
            P(),
            rows,
            rows,
            P("seq", None, None, ("x", "core")),
            P("seq", ("x", "core"), None),
        ),
        out_specs=rows,
        check_vma=False,
    )
```

```python
import functools

import jax
import jax.numpy as jnp
from jax import lax
from jax.experimental import pallas as pl
from jax.experimental.pallas import tpu as pltpu
from jax.sharding import Mesh
from jax.sharding import PartitionSpec as P

F32, BF16 = (jnp.float32, jnp.bfloat16)
HEAD = 128
EXTRA = 8
MIB = 1 << 20
NT = (((1,), (1,)), ((), ()))
TN = (((0,), (0,)), ((), ()))


def vmem(count):
    return [pl.BlockSpec(memory_space=pltpu.VMEM)] * count


def whole_call(kernel, outs, args, flops, limit, scratch=(), in_place=()):
    moved = sum(a.size * a.dtype.itemsize for a in (*args, *outs))
    return pl.pallas_call(
        kernel,
        out_shape=outs,
        in_specs=[
            pl.BlockSpec(memory_space=pltpu.HBM if place in in_place else pltpu.VMEM)
            for place in range(len(args))
        ],
        out_specs=vmem(len(outs)),
        scratch_shapes=list(scratch),
        cost_estimate=pl.CostEstimate(flops=flops, bytes_accessed=moved, transcendentals=0),
        compiler_params=pltpu.CompilerParams(vmem_limit_bytes=limit * MIB),
    )(*args)


def lane_block(h):
    return slice(h * HEAD, (h + 1) * HEAD)


def state_kernel(
    rates_in_ref,
    key_rows_ref,
    value_rows_ref,
    sent_ref,
    by_head_ref,
    rates_ref,
    key_ref,
    value_ref,
    loaded,
    rates_loaded,
):
    heads, tokens = rates_ref.shape
    rates_copy = pltpu.make_async_copy(rates_in_ref, rates_ref, rates_loaded)
    rates_copy.start()
    groups = loaded.shape[1]
    columns = heads * HEAD // groups
    copies = [
        [
            pltpu.make_async_copy(
                source.at[:, pl.ds(g * columns, columns)],
                target.at[:, pl.ds(g * columns, columns)],
                loaded.at[place, g],
            )
            for place, (source, target) in enumerate(
                ((key_rows_ref, key_ref), (value_rows_ref, value_ref))
            )
        ]
        for g in range(groups)
    ]
    for pair in copies:
        for copy in pair:
            copy.start()
    rates_copy.wait()
    at = lambda dim: lax.broadcasted_iota(jnp.int32, (tokens, tokens), dim)
    upto = (at(0) <= at(1)).astype(F32)
    by_head = jnp.dot(
        rates_ref[...], upto, precision=lax.Precision.HIGHEST, preferred_element_type=F32
    )
    by_head_ref[...] = by_head
    fade = jnp.exp(by_head - by_head[:, tokens - 1 :])
    keep = jnp.broadcast_to(jnp.exp(-by_head[:, tokens - 1 :]), (heads, HEAD))
    high = keep.astype(BF16).astype(F32)
    middle = (keep - high).astype(BF16).astype(F32)
    low = keep - high - middle
    row = lax.broadcasted_iota(jnp.int32, (EXTRA, HEAD), 0)
    for h in range(heads):
        if h % (heads // groups) == 0:
            for copy in copies[h // (heads // groups)]:
                copy.wait()
        turned = key_ref[:, lane_block(h)].T
        faded = (turned.astype(F32) * fade[h : h + 1, :]).astype(BF16)
        state = jnp.dot(faded, value_ref[:, lane_block(h)], preferred_element_type=F32)
        tail = jnp.where(row == 0, high[h : h + 1], 0.0)
        tail = jnp.where(row == 1, middle[h : h + 1], tail)
        tail = jnp.where(row == 2, low[h : h + 1], tail).astype(BF16)
        sent_ref[h, :HEAD, :] = state.astype(BF16)
        sent_ref[h, HEAD:, :] = tail


def scan_kernel(arrived_ref, within_ref, kept_ref, total_ref):
    def step(block, carry):
        state, kept = carry
        within_ref[block] = state
        kept_ref[block] = kept
        tail = arrived_ref[block, HEAD:, :].astype(F32)
        keep = tail[0:1] + tail[1:2] + tail[2:3]
        return keep * state + arrived_ref[block, :HEAD, :].astype(F32), keep * kept

    start = (jnp.zeros((HEAD, HEAD), F32), jnp.ones((EXTRA, HEAD), F32))
    state, kept = lax.fori_loop(0, within_ref.shape[0], step, start, unroll=4)
    total_ref[:HEAD, :] = state
    total_ref[HEAD:, :] = kept


def carry_kernel(within_ref, kept_ref, earlier_ref, *rest):
    *total_refs, carried_ref = rest
    before = jnp.zeros((HEAD, HEAD), F32)
    for place, total_ref in reversed(list(enumerate(total_refs))):
        longer = total_ref[:HEAD, :] + total_ref[HEAD : HEAD + 1, :] * before
        before = jnp.where(earlier_ref[place : place + 1, :] > 0.0, longer, before)

    def step(block, _):
        carried = within_ref[block] + kept_ref[block, 0:1, :] * before
        carried_ref[block] = carried.astype(BF16)
        return 0

    lax.fori_loop(0, carried_ref.shape[0], step, 0, unroll=4)


def local_kernel(
    query_ref,
    key_ref,
    value_ref,
    by_head_ref,
    out_ref,
):
    heads, tokens = by_head_ref.shape
    by_token = by_head_ref[...].T
    at = lambda dim: lax.broadcasted_iota(jnp.int32, (tokens, tokens), dim)
    causal = at(0) >= at(1)
    for h in range(heads):
        scores = lax.dot_general(
            query_ref[:, lane_block(h)], key_ref[:, lane_block(h)], NT, preferred_element_type=F32
        )
        spacing = by_head_ref[h : h + 1, :] - by_token[:, h : h + 1]
        fading = jnp.exp(jnp.minimum(spacing, 0.0))
        weights = jnp.where(causal, scores * fading, 0.0).astype(BF16)
        out_ref[:, lane_block(h)] = jnp.dot(
            weights, value_ref[:, lane_block(h)], preferred_element_type=F32
        )


def places(index_ref, experts):
    tokens = index_ref.shape[1]
    expert = lax.broadcasted_iota(jnp.int32, (experts, tokens), 0)
    first, second = (index_ref[0:1, :] == expert, index_ref[1:2, :] == expert)
    named = (first | second).astype(F32)
    at = lambda dim: lax.broadcasted_iota(jnp.int32, (tokens, tokens), dim)
    earlier = (at(0) < at(1)).astype(BF16)
    slot = jnp.dot(named.astype(BF16), earlier, preferred_element_type=F32)
    return first, second, jnp.where(named > 0.0, slot, -1.0)


def chunk_rows(slot, chunk, rows):
    experts, tokens = slot.shape
    wanted = lax.broadcasted_iota(jnp.int32, (rows, tokens), 0).astype(F32) + float(chunk * rows)
    return [slot[e : e + 1, :] == wanted for e in range(experts)]


def stream_kernel(
    query_ref,
    local_ref,
    gate_ref,
    residual_ref,
    carried_ref,
    by_head_ref,
    attention_gain_ref,
    expert_gain_ref,
    index_ref,
    stream_ref,
    *rest,
):
    *bin_refs, attention_ref = rest
    tokens, width = query_ref.shape
    heads = width // HEAD
    since = jnp.exp(-by_head_ref[...]).T
    total = jnp.zeros((tokens, HEAD), F32)
    for h in range(heads):
        carried_out = jnp.dot(
            query_ref[:, lane_block(h)], carried_ref[h], preferred_element_type=F32
        )
        attention = local_ref[:, lane_block(h)] + since[:, h : h + 1] * carried_out
        attention_ref[:, lane_block(h)] = attention
        total = total + attention * attention
    inverse = lax.rsqrt(jnp.sum(total, axis=1, keepdims=True) / width + 1e-05)
    total = jnp.zeros((tokens, HEAD), F32)
    for h in range(heads):
        gate = gate_ref[:, lane_block(h)].astype(F32)
        gain = attention_gain_ref[:, lane_block(h)] / (1.0 + jnp.exp(-gate))
        gated = attention_ref[:, lane_block(h)] * inverse * gain
        stream = (residual_ref[:, lane_block(h)].astype(F32) + gated).astype(BF16)
        stream_ref[:, lane_block(h)] = stream
        wide = stream.astype(F32)
        total = total + wide * wide
    inverse = lax.rsqrt(jnp.sum(total, axis=1, keepdims=True) / width + 1e-05)
    experts = bin_refs[0].shape[0]
    rows = bin_refs[0].shape[1]
    slot = places(index_ref, experts)[2]
    selectors = [
        jnp.concatenate([m.astype(F32) for m in chunk_rows(slot, c, rows)], axis=0).astype(BF16)
        for c in range(len(bin_refs))
    ]
    for h in range(heads):
        wide = stream_ref[:, lane_block(h)].astype(F32)
        entry = (wide * inverse * expert_gain_ref[:, lane_block(h)]).astype(BF16)
        for selector, bin_ref in zip(selectors, bin_refs):
            picked = jnp.dot(selector, entry, preferred_element_type=F32)
            bin_ref[:, :, lane_block(h)] = picked.astype(BF16).reshape(experts, rows, HEAD)


def mix_kernel(stream_ref, index_ref, router_ref, *rest):
    *returned_refs, out_ref = rest
    experts, rows, width = returned_refs[0].shape
    first, second, slot = places(index_ref, experts)
    scale = jnp.where(first, router_ref[0:1, :], 0.0) + jnp.where(second, router_ref[1:2, :], 0.0)
    weights = []
    for c in range(len(returned_refs)):
        masks = chunk_rows(slot, c, rows)
        chosen = jnp.concatenate(
            [jnp.where(m, scale[e : e + 1, :], 0.0) for e, m in enumerate(masks)], axis=0
        ).T
        high = chosen.astype(BF16)
        weights.append((high, (chosen - high.astype(F32)).astype(BF16)))
    for h in range(width // HEAD // 4):
        columns = slice(h * 4 * HEAD, (h + 1) * 4 * HEAD)
        total = stream_ref[:, columns].astype(F32)
        for (high, low), returned_ref in zip(weights, returned_refs):
            returned = returned_ref[:, :, columns].reshape(experts * rows, 4 * HEAD)
            total = total + jnp.dot(high, returned, preferred_element_type=F32)
            total = total + jnp.dot(low, returned, preferred_element_type=F32)
        out_ref[:, columns] = total.astype(BF16)


def expert_kernel(
    own_ref,
    left_ref,
    right_ref,
    far_ref,
    up_own_ref,
    up_other_ref,
    down_own_ref,
    down_other_ref,
    out_own_ref,
    out_left_ref,
    out_right_ref,
    out_far_ref,
    rows_ref,
    up_ref,
    down_ref,
    turned_ref,
    hidden_ref,
    up_sem,
    down_sem,
):
    count = own_ref.shape[0]
    tiles, _, tile, width = up_ref.shape
    units = down_own_ref.shape[0]
    parts, _, columns = down_ref.shape
    each = tiles // 2

    def up_copies(k):
        source = (up_own_ref, up_other_ref)[k // each]
        part = source.at[:, pl.ds(k % each * tile, tile), :]
        return [pltpu.make_async_copy(part, up_ref.at[k], up_sem.at[k])]

    def down_copies(k):
        return [
            pltpu.make_async_copy(
                source.at[:, pl.ds(k * columns, columns)],
                down_ref.at[k, pl.ds(place * units, units), :],
                down_sem.at[k, place],
            )
            for place, source in enumerate((down_own_ref, down_other_ref))
        ]

    loads = [up_copies(k) for k in range(tiles)] + [down_copies(k) for k in range(parts)]
    in_flight = 2

    def start(k):
        if k < len(loads):
            for copy in loads[k]:
                copy.start()

    def arrive(k):
        for copy in loads[k]:
            copy.wait()
        start(k + in_flight)

    for k in range(in_flight):
        start(k)
    rows_ref[0:count] = own_ref[...]
    rows_ref[count : 2 * count] = left_ref[...]
    rows_ref[2 * count : 3 * count] = right_ref[...]
    rows_ref[3 * count :] = far_ref[...]
    for k in range(tiles):
        arrive(k)
        both = up_ref[k].reshape(2 * tile, width)
        pair = lax.dot_general(both, rows_ref[...], NT, preferred_element_type=F32)
        gate, up = (pair[:tile], pair[tile:])
        hidden = gate / (1.0 + jnp.exp(-gate)) * up
        turned_ref[k * tile : (k + 1) * tile, :] = hidden.astype(BF16)
    hidden_ref[...] = turned_ref[...].T
    for k in range(parts):
        arrive(tiles + k)
        out = jnp.dot(hidden_ref[...], down_ref[k], preferred_element_type=F32).astype(BF16)
        for place, ref in enumerate((out_own_ref, out_left_ref, out_right_ref, out_far_ref)):
            ref[:, k * columns : (k + 1) * columns] = out[place * count : (place + 1) * count]


def expert_rows(blocks, up_own, up_other, down_own, down_other):
    count, width = blocks[0].shape
    units = down_own.shape[0]
    tiles, parts = (4, 4)
    tile, columns = (2 * units // tiles, width // parts)
    in_place = [pl.BlockSpec(memory_space=pltpu.HBM)] * 4
    return pl.pallas_call(
        expert_kernel,
        in_specs=vmem(len(blocks)) + in_place,
        out_specs=vmem(4),
        out_shape=[jax.ShapeDtypeStruct((count, width), BF16)] * 4,
        scratch_shapes=[
            pltpu.VMEM((4 * count, width), BF16),
            pltpu.VMEM((tiles, 2, tile, width), BF16),
            pltpu.VMEM((parts, 2 * units, columns), BF16),
            pltpu.VMEM((2 * units, 4 * count), BF16),
            pltpu.VMEM((4 * count, 2 * units), BF16),
            pltpu.SemaphoreType.DMA((tiles,)),
            pltpu.SemaphoreType.DMA((parts, 2)),
        ],
        cost_estimate=pl.CostEstimate(
            flops=4 * count * 2 * units * width * 6,
            bytes_accessed=6 * units * width * 2 + 8 * count * width * 2,
            transcendentals=0,
        ),
        compiler_params=pltpu.CompilerParams(vmem_limit_bytes=46 * MIB),
    )(*blocks, up_own, up_other, down_own, down_other)


def body(
    queries,
    key_rows,
    value_rows,
    gate_logits,
    residual_in,
    decay_rate,
    attention_gain,
    expert_gain,
    expert_index,
    router_weight,
    gate_up_weight,
    down_weight,
):
    chips, experts = (lax.axis_size("x"), lax.axis_size("seq"))
    tokens, width = queries.shape
    heads = decay_rate.shape[1]
    chunks = 2
    slots = tokens * expert_index.shape[1] // experts
    rows = slots // chunks
    count = experts * rows

    swap = lambda a: lax.ppermute(a, "core", [(0, 1), (1, 0)])
    go_ahead = lambda a: lax.ppermute(a, "x", [(i, (i + 1) % chips) for i in range(chips)])
    go_back = lambda a: lax.ppermute(a, "x", [(i, (i - 1) % chips) for i in range(chips)])
    to_later = lambda a, k: lax.ppermute(a, "x", [(i, (i + k) % chips) for i in range(chips)])
    plane = ("core", "seq")
    after = lambda value, *earlier: lax.optimization_barrier((value, earlier))[0]
    exchange = lambda a, axis: lax.all_to_all(a, axis, split_axis=0, concat_axis=0, tiled=True)
    shape = jax.ShapeDtypeStruct

    up_own = jnp.transpose(gate_up_weight[0], (1, 2, 0))
    down_own = down_weight[0]

    sent, by_head = whole_call(
        state_kernel,
        [
            shape((heads, HEAD + EXTRA, HEAD), BF16),
            shape((heads, tokens), F32),
        ],
        [decay_rate.T, key_rows, value_rows],
        2 * tokens * width * HEAD,
        62,
        [
            pltpu.VMEM((heads, tokens), F32),
            pltpu.VMEM((tokens, width), BF16),
            pltpu.VMEM((tokens, width), BF16),
            pltpu.SemaphoreType.DMA((2, 4)),
            pltpu.SemaphoreType.DMA,
        ],
        (0, 1, 2),
    )
    arrived = exchange(sent, plane)
    (local_out,) = whole_call(
        local_kernel,
        [shape((tokens, width), F32)],
        [queries, key_rows, value_rows, by_head],
        4 * tokens * width * tokens,
        16,
    )
    within, kept, total = whole_call(
        scan_kernel,
        [
            shape((heads, HEAD, HEAD), F32),
            shape((heads, EXTRA, HEAD), F32),
            shape((HEAD + EXTRA, HEAD), F32),
        ],
        [after(arrived, local_out)],
        2 * heads * HEAD * HEAD,
        8,
    )
    distance = lax.broadcasted_iota(jnp.int32, (chips - 1, HEAD), 0) + 1
    earlier = (distance <= lax.axis_index("x")).astype(F32)
    totals = [to_later(total, k) for k in range(1, chips)]
    (carried,) = whole_call(
        carry_kernel,
        [shape((heads, HEAD, HEAD), BF16)],
        [within, kept, earlier, *totals],
        2 * heads * HEAD * HEAD,
        8,
    )
    carried_low = exchange(carried, plane)
    index = expert_index.T
    stream, *bins = whole_call(
        stream_kernel,
        [shape((tokens, width), BF16)] + [shape((experts, rows, width), BF16)] * chunks,
        [
            queries,
            local_out,
            gate_logits,
            residual_in,
            carried_low,
            by_head,
            attention_gain[None, :],
            expert_gain[None, :],
            index,
        ],
        2 * tokens * width * (HEAD + chunks * count),
        8,
        [pltpu.VMEM((tokens, width), F32)],
    )

    up_other = swap(after(up_own, stream))
    down_other = swap(after(down_own, stream))
    weights = (up_own, up_other, down_own, down_other)
    wide = lambda a: a.astype(F32)
    plus = lambda *terms: functools.reduce(jnp.add, map(wide, terms)).astype(BF16)

    own_a, own_b = (exchange(bin_rows, "seq").reshape(count, width) for bin_rows in bins)
    left_a, right_a = (go_ahead(own_a), go_back(own_a))
    far_a = go_ahead(after(left_a, own_b))
    right_b = go_back(after(own_b, right_a, down_other))
    left_b = go_ahead(after(own_b, far_a))
    far_b = go_back(right_b)
    out_own_a, out_left_a, out_right_a, out_far_a = expert_rows(
        (own_a, left_a, right_a, far_a), *weights
    )
    pass_a, back_a = (go_ahead(out_far_a), go_back(out_left_a))
    out_own_b, out_left_b, out_right_b, out_far_b = expert_rows(
        (own_b, left_b, right_b, far_b), *weights
    )
    pass_b = go_back(after(out_far_b, pass_a, back_a))
    ahead_a = go_ahead(plus(out_right_a, pass_a))
    ahead_b = go_ahead(after(out_right_b, ahead_a))
    to_left_b = plus(out_left_b, pass_b)
    back_b = go_back(to_left_b)
    home = lambda *terms: plus(*terms).reshape(experts, rows, width)
    returned_a = exchange(after(home(out_own_a, ahead_a, back_a), to_left_b), "seq")
    returned_b = exchange(home(after(out_own_b, returned_a), ahead_b, back_b), "seq")
    (out,) = whole_call(
        mix_kernel,
        [shape((tokens, width), BF16)],
        [stream, index, router_weight.T, returned_a, returned_b],
        4 * tokens * width * count * chunks,
        16,
    )
    return out


def solution(mesh):
    groups, experts = (mesh.shape["grp"], mesh.shape["seq"])
    split = Mesh(mesh.devices.reshape(groups // 2, 2, experts), ("x", "core", "seq"))
    rows = P(("x", "core", "seq"), None)
    return jax.shard_map(
        body,
        mesh=split,
        in_specs=(
            rows,
            rows,
            rows,
            rows,
            rows,
            rows,
            P(),
            P(),
            rows,
            rows,
            P("seq", None, None, ("x", "core")),
            P("seq", ("x", "core"), None),
        ),
        out_specs=rows,
        check_vma=False,
    )
```

```python
import functools

import jax
import jax.numpy as jnp
from jax import lax
from jax.experimental import pallas as pl
from jax.experimental.pallas import tpu as pltpu
from jax.sharding import Mesh
from jax.sharding import PartitionSpec as P

F32, BF16 = (jnp.float32, jnp.bfloat16)
HEAD = 128
EXTRA = 8
MIB = 1 << 20
NT = (((1,), (1,)), ((), ()))
TN = (((0,), (0,)), ((), ()))


def vmem(count):
    return [pl.BlockSpec(memory_space=pltpu.VMEM)] * count


def whole_call(kernel, outs, args, flops, limit, scratch=(), in_place=(), out_in_place=()):
    moved = sum(a.size * a.dtype.itemsize for a in (*args, *outs))
    return pl.pallas_call(
        kernel,
        out_shape=outs,
        in_specs=[
            pl.BlockSpec(memory_space=pltpu.HBM if place in in_place else pltpu.VMEM)
            for place in range(len(args))
        ],
        out_specs=[
            pl.BlockSpec(memory_space=pltpu.HBM if place in out_in_place else pltpu.VMEM)
            for place in range(len(outs))
        ],
        scratch_shapes=list(scratch),
        cost_estimate=pl.CostEstimate(flops=flops, bytes_accessed=moved, transcendentals=0),
        compiler_params=pltpu.CompilerParams(vmem_limit_bytes=limit * MIB),
    )(*args)


def lane_block(h):
    return slice(h * HEAD, (h + 1) * HEAD)


def state_kernel(
    rates_in_ref,
    key_rows_ref,
    value_rows_ref,
    sent_ref,
    by_head_ref,
    rates_ref,
    key_ref,
    value_ref,
    loaded,
    rates_loaded,
):
    heads, tokens = rates_ref.shape
    rates_copy = pltpu.make_async_copy(rates_in_ref, rates_ref, rates_loaded)
    rates_copy.start()
    groups = loaded.shape[1]
    columns = heads * HEAD // groups
    copies = [
        [
            pltpu.make_async_copy(
                source.at[:, pl.ds(g * columns, columns)],
                target.at[:, pl.ds(g * columns, columns)],
                loaded.at[place, g],
            )
            for place, (source, target) in enumerate(
                ((key_rows_ref, key_ref), (value_rows_ref, value_ref))
            )
        ]
        for g in range(groups)
    ]
    for pair in copies:
        for copy in pair:
            copy.start()
    rates_copy.wait()
    at = lambda dim: lax.broadcasted_iota(jnp.int32, (tokens, tokens), dim)
    upto = (at(0) <= at(1)).astype(F32)
    by_head = jnp.dot(
        rates_ref[...], upto, precision=lax.Precision.HIGHEST, preferred_element_type=F32
    )
    by_head_ref[...] = by_head
    fade = jnp.exp(by_head - by_head[:, tokens - 1 :])
    keep = jnp.broadcast_to(jnp.exp(-by_head[:, tokens - 1 :]), (heads, HEAD))
    high = keep.astype(BF16).astype(F32)
    middle = (keep - high).astype(BF16).astype(F32)
    low = keep - high - middle
    row = lax.broadcasted_iota(jnp.int32, (EXTRA, HEAD), 0)
    for h in range(heads):
        if h % (heads // groups) == 0:
            for copy in copies[h // (heads // groups)]:
                copy.wait()
        turned = key_ref[:, lane_block(h)].T
        faded = (turned.astype(F32) * fade[h : h + 1, :]).astype(BF16)
        state = jnp.dot(faded, value_ref[:, lane_block(h)], preferred_element_type=F32)
        tail = jnp.where(row == 0, high[h : h + 1], 0.0)
        tail = jnp.where(row == 1, middle[h : h + 1], tail)
        tail = jnp.where(row == 2, low[h : h + 1], tail).astype(BF16)
        sent_ref[h, :HEAD, :] = state.astype(BF16)
        sent_ref[h, HEAD:, :] = tail


def scan_kernel(arrived_ref, within_ref, kept_ref, total_ref):
    def step(block, carry):
        state, kept = carry
        within_ref[block] = state
        kept_ref[block] = kept
        tail = arrived_ref[block, HEAD:, :].astype(F32)
        keep = tail[0:1] + tail[1:2] + tail[2:3]
        return keep * state + arrived_ref[block, :HEAD, :].astype(F32), keep * kept

    start = (jnp.zeros((HEAD, HEAD), F32), jnp.ones((EXTRA, HEAD), F32))
    state, kept = lax.fori_loop(0, within_ref.shape[0], step, start, unroll=4)
    total_ref[:HEAD, :] = state.astype(BF16)
    high = kept.astype(BF16).astype(F32)
    middle = (kept - high).astype(BF16).astype(F32)
    row = lax.broadcasted_iota(jnp.int32, kept.shape, 0)
    tail = jnp.where(row == 0, high, jnp.where(row == 1, middle, kept - high - middle))
    total_ref[HEAD:, :] = tail.astype(BF16)


def carry_kernel(within_ref, kept_ref, earlier_ref, *rest):
    *total_refs, carried_ref = rest
    before = jnp.zeros((HEAD, HEAD), F32)
    for place, total_ref in reversed(list(enumerate(total_refs))):
        tail = total_ref[HEAD:, :].astype(F32)
        keep = tail[0:1] + tail[1:2] + tail[2:3]
        longer = total_ref[:HEAD, :].astype(F32) + keep * before
        before = jnp.where(earlier_ref[place : place + 1, :] > 0.0, longer, before)

    def step(block, _):
        carried = within_ref[block] + kept_ref[block, 0:1, :] * before
        carried_ref[block] = carried.astype(BF16)
        return 0

    lax.fori_loop(0, carried_ref.shape[0], step, 0, unroll=4)


def local_kernel(
    query_ref,
    key_ref,
    value_ref,
    by_head_ref,
    out_ref,
):
    heads, tokens = by_head_ref.shape
    by_token = by_head_ref[...].T
    at = lambda dim: lax.broadcasted_iota(jnp.int32, (tokens, tokens), dim)
    causal = at(0) >= at(1)
    for h in range(heads):
        scores = lax.dot_general(
            query_ref[:, lane_block(h)], key_ref[:, lane_block(h)], NT, preferred_element_type=F32
        )
        spacing = by_head_ref[h : h + 1, :] - by_token[:, h : h + 1]
        fading = jnp.exp(jnp.minimum(spacing, 0.0))
        weights = jnp.where(causal, scores * fading, 0.0).astype(BF16)
        out_ref[:, lane_block(h)] = jnp.dot(
            weights, value_ref[:, lane_block(h)], preferred_element_type=F32
        )


def places(index_ref, experts):
    tokens = index_ref.shape[1]
    expert = lax.broadcasted_iota(jnp.int32, (experts, tokens), 0)
    first, second = (index_ref[0:1, :] == expert, index_ref[1:2, :] == expert)
    named = (first | second).astype(F32)
    at = lambda dim: lax.broadcasted_iota(jnp.int32, (tokens, tokens), dim)
    earlier = (at(0) < at(1)).astype(BF16)
    slot = jnp.dot(named.astype(BF16), earlier, preferred_element_type=F32)
    return first, second, jnp.where(named > 0.0, slot, -1.0)


def chunk_rows(slot, chunk, rows):
    experts, tokens = slot.shape
    wanted = lax.broadcasted_iota(jnp.int32, (rows, tokens), 0).astype(F32) + float(chunk * rows)
    return [slot[e : e + 1, :] == wanted for e in range(experts)]


def stream_kernel(
    query_ref,
    local_ref,
    gate_ref,
    residual_ref,
    carried_ref,
    by_head_ref,
    attention_gain_ref,
    expert_gain_ref,
    index_ref,
    stream_ref,
    *rest,
):
    *bin_refs, attention_ref = rest
    tokens, width = query_ref.shape
    heads = width // HEAD
    since = jnp.exp(-by_head_ref[...]).T
    total = jnp.zeros((tokens, HEAD), F32)
    for h in range(heads):
        carried_out = jnp.dot(
            query_ref[:, lane_block(h)], carried_ref[h], preferred_element_type=F32
        )
        attention = local_ref[:, lane_block(h)] + since[:, h : h + 1] * carried_out
        attention_ref[:, lane_block(h)] = attention
        total = total + attention * attention
    inverse = lax.rsqrt(jnp.sum(total, axis=1, keepdims=True) / width + 1e-05)
    total = jnp.zeros((tokens, HEAD), F32)
    for h in range(heads):
        gate = gate_ref[:, lane_block(h)].astype(F32)
        gain = attention_gain_ref[:, lane_block(h)] / (1.0 + jnp.exp(-gate))
        gated = attention_ref[:, lane_block(h)] * inverse * gain
        stream = (residual_ref[:, lane_block(h)].astype(F32) + gated).astype(BF16)
        stream_ref[:, lane_block(h)] = stream
        wide = stream.astype(F32)
        total = total + wide * wide
    inverse = lax.rsqrt(jnp.sum(total, axis=1, keepdims=True) / width + 1e-05)
    experts = bin_refs[0].shape[0]
    rows = bin_refs[0].shape[1]
    slot = places(index_ref, experts)[2]
    selectors = [
        jnp.concatenate([m.astype(F32) for m in chunk_rows(slot, c, rows)], axis=0).astype(BF16)
        for c in range(len(bin_refs))
    ]
    for h in range(heads):
        wide = stream_ref[:, lane_block(h)].astype(F32)
        entry = (wide * inverse * expert_gain_ref[:, lane_block(h)]).astype(BF16)
        for selector, bin_ref in zip(selectors, bin_refs):
            picked = jnp.dot(selector, entry, preferred_element_type=F32)
            bin_ref[:, :, lane_block(h)] = picked.astype(BF16).reshape(experts, rows, HEAD)


def first_mix_kernel(
    stream_ref, index_ref, router_ref, returned_ref, total_ref, later_high_ref, later_low_ref
):
    experts, rows, width = returned_ref.shape
    first, second, slot = places(index_ref, experts)
    scale = jnp.where(first, router_ref[0:1, :], 0.0) + jnp.where(second, router_ref[1:2, :], 0.0)
    weights = []
    for c in range(2):
        masks = chunk_rows(slot, c, rows)
        chosen = jnp.concatenate(
            [jnp.where(m, scale[e : e + 1, :], 0.0) for e, m in enumerate(masks)], axis=0
        ).T
        high = chosen.astype(BF16)
        weights.append((high, (chosen - high.astype(F32)).astype(BF16)))
    later_high_ref[...], later_low_ref[...] = weights[1]
    high, low = weights[0]
    for h in range(width // HEAD // 4):
        columns = slice(h * 4 * HEAD, (h + 1) * 4 * HEAD)
        returned = returned_ref[:, :, columns].reshape(experts * rows, 4 * HEAD)
        total = stream_ref[:, columns].astype(F32)
        total = total + jnp.dot(high, returned, preferred_element_type=F32)
        total_ref[:, columns] = total + jnp.dot(low, returned, preferred_element_type=F32)


def last_mix_kernel(total_ref, high_ref, low_ref, returned_ref, out_ref, mixed_ref, stored):
    experts, rows, width = returned_ref.shape
    groups = stored.shape[0]
    size = width // groups
    copies = []
    for g in range(groups):
        columns = slice(g * size, (g + 1) * size)
        returned = returned_ref[:, :, columns].reshape(experts * rows, size)
        total = total_ref[:, columns]
        total = total + jnp.dot(high_ref[...], returned, preferred_element_type=F32)
        total = total + jnp.dot(low_ref[...], returned, preferred_element_type=F32)
        mixed_ref[:, columns] = total.astype(BF16)
        part = pl.ds(g * size, size)
        copies.append(
            pltpu.make_async_copy(mixed_ref.at[:, part], out_ref.at[:, part], stored.at[g])
        )
        copies[-1].start()
    for copy in copies:
        copy.wait()


def expert_kernel(
    own_ref,
    left_ref,
    right_ref,
    far_ref,
    up_own_ref,
    up_other_ref,
    down_own_ref,
    down_other_ref,
    out_own_ref,
    out_left_ref,
    out_right_ref,
    out_far_ref,
    rows_ref,
    up_ref,
    down_ref,
    turned_ref,
    hidden_ref,
    up_sem,
    down_sem,
):
    count = own_ref.shape[0]
    tiles, _, tile, width = up_ref.shape
    units = down_own_ref.shape[0]
    parts, _, columns = down_ref.shape
    each = tiles // 2

    def up_copies(k):
        source = (up_own_ref, up_other_ref)[k // each]
        part = source.at[:, pl.ds(k % each * tile, tile), :]
        return [pltpu.make_async_copy(part, up_ref.at[k], up_sem.at[k])]

    def down_copies(k):
        return [
            pltpu.make_async_copy(
                source.at[:, pl.ds(k * columns, columns)],
                down_ref.at[k, pl.ds(place * units, units), :],
                down_sem.at[k, place],
            )
            for place, source in enumerate((down_own_ref, down_other_ref))
        ]

    loads = [up_copies(k) for k in range(tiles)] + [down_copies(k) for k in range(parts)]
    in_flight = 2

    def start(k):
        if k < len(loads):
            for copy in loads[k]:
                copy.start()

    def arrive(k):
        for copy in loads[k]:
            copy.wait()
        start(k + in_flight)

    for k in range(in_flight):
        start(k)
    rows_ref[0:count] = own_ref[...]
    rows_ref[count : 2 * count] = left_ref[...]
    rows_ref[2 * count : 3 * count] = right_ref[...]
    rows_ref[3 * count :] = far_ref[...]
    for k in range(tiles):
        arrive(k)
        both = up_ref[k].reshape(2 * tile, width)
        pair = lax.dot_general(both, rows_ref[...], NT, preferred_element_type=F32)
        gate, up = (pair[:tile], pair[tile:])
        hidden = gate / (1.0 + jnp.exp(-gate)) * up
        turned_ref[k * tile : (k + 1) * tile, :] = hidden.astype(BF16)
    hidden_ref[...] = turned_ref[...].T
    for k in range(parts):
        arrive(tiles + k)
        out = jnp.dot(hidden_ref[...], down_ref[k], preferred_element_type=F32).astype(BF16)
        for place, ref in enumerate((out_own_ref, out_left_ref, out_right_ref, out_far_ref)):
            ref[:, k * columns : (k + 1) * columns] = out[place * count : (place + 1) * count]


def expert_rows(blocks, up_own, up_other, down_own, down_other):
    count, width = blocks[0].shape
    units = down_own.shape[0]
    tiles, parts = (4, 4)
    tile, columns = (2 * units // tiles, width // parts)
    in_place = [pl.BlockSpec(memory_space=pltpu.HBM)] * 4
    return pl.pallas_call(
        expert_kernel,
        in_specs=vmem(len(blocks)) + in_place,
        out_specs=vmem(4),
        out_shape=[jax.ShapeDtypeStruct((count, width), BF16)] * 4,
        scratch_shapes=[
            pltpu.VMEM((4 * count, width), BF16),
            pltpu.VMEM((tiles, 2, tile, width), BF16),
            pltpu.VMEM((parts, 2 * units, columns), BF16),
            pltpu.VMEM((2 * units, 4 * count), BF16),
            pltpu.VMEM((4 * count, 2 * units), BF16),
            pltpu.SemaphoreType.DMA((tiles,)),
            pltpu.SemaphoreType.DMA((parts, 2)),
        ],
        cost_estimate=pl.CostEstimate(
            flops=4 * count * 2 * units * width * 6,
            bytes_accessed=6 * units * width * 2 + 8 * count * width * 2,
            transcendentals=0,
        ),
        compiler_params=pltpu.CompilerParams(vmem_limit_bytes=46 * MIB),
    )(*blocks, up_own, up_other, down_own, down_other)


def body(
    queries,
    key_rows,
    value_rows,
    gate_logits,
    residual_in,
    decay_rate,
    attention_gain,
    expert_gain,
    expert_index,
    router_weight,
    gate_up_weight,
    down_weight,
):
    chips, experts = (lax.axis_size("x"), lax.axis_size("seq"))
    tokens, width = queries.shape
    heads = decay_rate.shape[1]
    chunks = 2
    slots = tokens * expert_index.shape[1] // experts
    rows = slots // chunks
    count = experts * rows

    swap = lambda a: lax.ppermute(a, "core", [(0, 1), (1, 0)])
    go_ahead = lambda a: lax.ppermute(a, "x", [(i, (i + 1) % chips) for i in range(chips)])
    go_back = lambda a: lax.ppermute(a, "x", [(i, (i - 1) % chips) for i in range(chips)])
    to_later = lambda a, k: lax.ppermute(a, "x", [(i, (i + k) % chips) for i in range(chips)])
    plane = ("core", "seq")
    after = lambda value, *earlier: lax.optimization_barrier((value, earlier))[0]
    exchange = lambda a, axis: lax.all_to_all(a, axis, split_axis=0, concat_axis=0, tiled=True)
    shape = jax.ShapeDtypeStruct

    up_own = jnp.transpose(gate_up_weight[0], (1, 2, 0))
    down_own = down_weight[0]

    sent, by_head = whole_call(
        state_kernel,
        [
            shape((heads, HEAD + EXTRA, HEAD), BF16),
            shape((heads, tokens), F32),
        ],
        [decay_rate.T, key_rows, value_rows],
        2 * tokens * width * HEAD,
        62,
        [
            pltpu.VMEM((heads, tokens), F32),
            pltpu.VMEM((tokens, width), BF16),
            pltpu.VMEM((tokens, width), BF16),
            pltpu.SemaphoreType.DMA((2, 4)),
            pltpu.SemaphoreType.DMA,
        ],
        (0, 1, 2),
    )
    arrived = exchange(sent, plane)
    (local_out,) = whole_call(
        local_kernel,
        [shape((tokens, width), F32)],
        [queries, key_rows, value_rows, by_head],
        4 * tokens * width * tokens,
        16,
    )
    within, kept, total = whole_call(
        scan_kernel,
        [
            shape((heads, HEAD, HEAD), F32),
            shape((heads, EXTRA, HEAD), F32),
            shape((HEAD + EXTRA, HEAD), BF16),
        ],
        [after(arrived, local_out)],
        2 * heads * HEAD * HEAD,
        8,
    )
    distance = lax.broadcasted_iota(jnp.int32, (chips - 1, HEAD), 0) + 1
    earlier = (distance <= lax.axis_index("x")).astype(F32)
    totals = [to_later(total, k) for k in range(1, chips)]
    (carried,) = whole_call(
        carry_kernel,
        [shape((heads, HEAD, HEAD), BF16)],
        [within, kept, earlier, *totals],
        2 * heads * HEAD * HEAD,
        8,
    )
    carried_low = exchange(carried, plane)
    index = expert_index.T
    stream, *bins = whole_call(
        stream_kernel,
        [shape((tokens, width), BF16)] + [shape((experts, rows, width), BF16)] * chunks,
        [
            queries,
            local_out,
            gate_logits,
            residual_in,
            carried_low,
            by_head,
            attention_gain[None, :],
            expert_gain[None, :],
            index,
        ],
        2 * tokens * width * (HEAD + chunks * count),
        8,
        [pltpu.VMEM((tokens, width), F32)],
    )

    up_other = swap(after(up_own, stream))
    down_other = swap(after(down_own, stream))
    weights = (up_own, up_other, down_own, down_other)
    wide = lambda a: a.astype(F32)
    plus = lambda *terms: functools.reduce(jnp.add, map(wide, terms)).astype(BF16)

    own_a, own_b = (exchange(bin_rows, "seq").reshape(count, width) for bin_rows in bins)
    left_a, right_a = (go_ahead(own_a), go_back(own_a))
    far_a = go_ahead(after(left_a, own_b))
    right_b = go_back(after(own_b, right_a, down_other))
    left_b = go_ahead(after(own_b, far_a))
    far_b = go_back(right_b)
    out_own_a, out_left_a, out_right_a, out_far_a = expert_rows(
        (own_a, left_a, right_a, far_a), *weights
    )
    pass_a, back_a = (go_ahead(out_far_a), go_back(out_left_a))
    out_own_b, out_left_b, out_right_b, out_far_b = expert_rows(
        (own_b, left_b, right_b, far_b), *weights
    )
    pass_b = go_back(after(out_far_b, pass_a, back_a))
    ahead_a = go_ahead(plus(out_right_a, pass_a))
    ahead_b = go_ahead(after(out_right_b, ahead_a))
    to_left_b = plus(out_left_b, pass_b)
    back_b = go_back(to_left_b)
    home = lambda *terms: plus(*terms).reshape(experts, rows, width)
    returned_a = exchange(after(home(out_own_a, ahead_a, back_a), to_left_b), "seq")
    total, high, low = whole_call(
        first_mix_kernel,
        [shape((tokens, width), F32)] + [shape((tokens, count), BF16)] * 2,
        [stream, index, router_weight.T, returned_a],
        4 * tokens * width * count,
        8,
    )
    returned_b = exchange(home(after(out_own_b, total), ahead_b, back_b), "seq")
    (out,) = whole_call(
        last_mix_kernel,
        [shape((tokens, width), BF16)],
        [total, high, low, returned_b],
        4 * tokens * width * count,
        8,
        [pltpu.VMEM((tokens, width), BF16), pltpu.SemaphoreType.DMA((4,))],
        out_in_place=(0,),
    )
    return out


def solution(mesh):
    groups, experts = (mesh.shape["grp"], mesh.shape["seq"])
    split = Mesh(mesh.devices.reshape(groups // 2, 2, experts), ("x", "core", "seq"))
    rows = P(("x", "core", "seq"), None)
    return jax.shard_map(
        body,
        mesh=split,
        in_specs=(
            rows,
            rows,
            rows,
            rows,
            rows,
            rows,
            P(),
            P(),
            rows,
            rows,
            P("seq", None, None, ("x", "core")),
            P("seq", ("x", "core"), None),
        ),
        out_specs=rows,
        check_vma=False,
    )
```

```python
import functools

import jax
import jax.numpy as jnp
from jax import lax
from jax.experimental import pallas as pl
from jax.experimental.pallas import tpu as pltpu
from jax.sharding import Mesh
from jax.sharding import PartitionSpec as P

F32, BF16 = (jnp.float32, jnp.bfloat16)
HEAD = 128
EXTRA = 8
MIB = 1 << 20
NT = (((1,), (1,)), ((), ()))
TN = (((0,), (0,)), ((), ()))


def vmem(count):
    return [pl.BlockSpec(memory_space=pltpu.VMEM)] * count


def whole_call(kernel, outs, args, flops, limit, scratch=(), in_place=(), out_in_place=()):
    moved = sum(a.size * a.dtype.itemsize for a in (*args, *outs))
    return pl.pallas_call(
        kernel,
        out_shape=outs,
        in_specs=[
            pl.BlockSpec(memory_space=pltpu.HBM if place in in_place else pltpu.VMEM)
            for place in range(len(args))
        ],
        out_specs=[
            pl.BlockSpec(memory_space=pltpu.HBM if place in out_in_place else pltpu.VMEM)
            for place in range(len(outs))
        ],
        scratch_shapes=list(scratch),
        cost_estimate=pl.CostEstimate(flops=flops, bytes_accessed=moved, transcendentals=0),
        compiler_params=pltpu.CompilerParams(vmem_limit_bytes=limit * MIB),
    )(*args)


def lane_block(h):
    return slice(h * HEAD, (h + 1) * HEAD)


def state_kernel(
    rates_in_ref,
    key_rows_ref,
    value_rows_ref,
    sent_ref,
    by_head_ref,
    rates_ref,
    key_ref,
    value_ref,
    loaded,
    rates_loaded,
):
    heads, tokens = rates_ref.shape
    rates_copy = pltpu.make_async_copy(rates_in_ref, rates_ref, rates_loaded)
    rates_copy.start()
    groups = loaded.shape[1]
    columns = heads * HEAD // groups
    copies = [
        [
            pltpu.make_async_copy(
                source.at[:, pl.ds(g * columns, columns)],
                target.at[:, pl.ds(g * columns, columns)],
                loaded.at[place, g],
            )
            for place, (source, target) in enumerate(
                ((key_rows_ref, key_ref), (value_rows_ref, value_ref))
            )
        ]
        for g in range(groups)
    ]
    for pair in copies:
        for copy in pair:
            copy.start()
    rates_copy.wait()
    at = lambda dim: lax.broadcasted_iota(jnp.int32, (tokens, tokens), dim)
    upto = (at(0) <= at(1)).astype(F32)
    by_head = jnp.dot(
        rates_ref[...], upto, precision=lax.Precision.HIGHEST, preferred_element_type=F32
    )
    by_head_ref[...] = by_head
    fade = jnp.exp(by_head - by_head[:, tokens - 1 :])
    keep = jnp.broadcast_to(jnp.exp(-by_head[:, tokens - 1 :]), (heads, HEAD))
    high = keep.astype(BF16).astype(F32)
    middle = (keep - high).astype(BF16).astype(F32)
    low = keep - high - middle
    row = lax.broadcasted_iota(jnp.int32, (EXTRA, HEAD), 0)
    for h in range(heads):
        if h % (heads // groups) == 0:
            for copy in copies[h // (heads // groups)]:
                copy.wait()
        turned = key_ref[:, lane_block(h)].T
        faded = (turned.astype(F32) * fade[h : h + 1, :]).astype(BF16)
        state = jnp.dot(faded, value_ref[:, lane_block(h)], preferred_element_type=F32)
        tail = jnp.where(row == 0, high[h : h + 1], 0.0)
        tail = jnp.where(row == 1, middle[h : h + 1], tail)
        tail = jnp.where(row == 2, low[h : h + 1], tail).astype(BF16)
        sent_ref[h, :HEAD, :] = state.astype(BF16)
        sent_ref[h, HEAD:, :] = tail


def scan_kernel(arrived_ref, within_ref, kept_ref, total_ref):
    def step(block, carry):
        state, kept = carry
        within_ref[block] = state
        kept_ref[block] = kept
        tail = arrived_ref[block, HEAD:, :].astype(F32)
        keep = tail[0:1] + tail[1:2] + tail[2:3]
        return keep * state + arrived_ref[block, :HEAD, :].astype(F32), keep * kept

    start = (jnp.zeros((HEAD, HEAD), F32), jnp.ones((EXTRA, HEAD), F32))
    state, kept = lax.fori_loop(0, within_ref.shape[0], step, start, unroll=4)
    total_ref[:HEAD, :] = state.astype(BF16)
    high = kept.astype(BF16).astype(F32)
    middle = (kept - high).astype(BF16).astype(F32)
    row = lax.broadcasted_iota(jnp.int32, kept.shape, 0)
    tail = jnp.where(row == 0, high, jnp.where(row == 1, middle, kept - high - middle))
    total_ref[HEAD:, :] = tail.astype(BF16)


def carry_kernel(within_ref, kept_ref, earlier_ref, *rest):
    *total_refs, carried_ref = rest
    before = jnp.zeros((HEAD, HEAD), F32)
    for place, total_ref in reversed(list(enumerate(total_refs))):
        tail = total_ref[HEAD:, :].astype(F32)
        keep = tail[0:1] + tail[1:2] + tail[2:3]
        longer = total_ref[:HEAD, :].astype(F32) + keep * before
        before = jnp.where(earlier_ref[place : place + 1, :] > 0.0, longer, before)

    def step(block, _):
        carried = within_ref[block] + kept_ref[block, 0:1, :] * before
        carried_ref[block] = carried.astype(BF16)
        return 0

    lax.fori_loop(0, carried_ref.shape[0], step, 0, unroll=4)


def local_kernel(
    experts,
    chunks,
    query_ref,
    key_ref,
    value_ref,
    by_head_ref,
    index_ref,
    gate_ref,
    attention_gain_ref,
    out_ref,
    since_ref,
    selector_ref,
    gate_gain_ref,
):
    heads, tokens = by_head_ref.shape
    by_token = by_head_ref[...].T
    since_ref[...] = jnp.exp(-by_token)
    slot = places(index_ref, experts)[2]
    count = selector_ref.shape[0] // chunks
    for c in range(chunks):
        masks = chunk_rows(slot, c, count // experts)
        selector = jnp.concatenate([m.astype(F32) for m in masks], axis=0)
        selector_ref[c * count : (c + 1) * count, :] = selector.astype(BF16)
    at = lambda dim: lax.broadcasted_iota(jnp.int32, (tokens, tokens), dim)
    causal = at(0) >= at(1)
    for h in range(heads):
        scores = lax.dot_general(
            query_ref[:, lane_block(h)], key_ref[:, lane_block(h)], NT, preferred_element_type=F32
        )
        spacing = by_head_ref[h : h + 1, :] - by_token[:, h : h + 1]
        fading = jnp.exp(jnp.minimum(spacing, 0.0))
        weights = jnp.where(causal, scores * fading, 0.0).astype(BF16)
        out_ref[:, lane_block(h)] = jnp.dot(
            weights, value_ref[:, lane_block(h)], preferred_element_type=F32
        )
        gate = gate_ref[:, lane_block(h)].astype(F32)
        gain = attention_gain_ref[:, lane_block(h)]
        gate_gain_ref[:, lane_block(h)] = gain / (1.0 + jnp.exp(-gate))


def places(index_ref, experts):
    tokens = index_ref.shape[1]
    expert = lax.broadcasted_iota(jnp.int32, (experts, tokens), 0)
    first, second = (index_ref[0:1, :] == expert, index_ref[1:2, :] == expert)
    named = (first | second).astype(F32)
    at = lambda dim: lax.broadcasted_iota(jnp.int32, (tokens, tokens), dim)
    earlier = (at(0) < at(1)).astype(BF16)
    slot = jnp.dot(named.astype(BF16), earlier, preferred_element_type=F32)
    return first, second, jnp.where(named > 0.0, slot, -1.0)


def chunk_rows(slot, chunk, rows):
    experts, tokens = slot.shape
    wanted = lax.broadcasted_iota(jnp.int32, (rows, tokens), 0).astype(F32) + float(chunk * rows)
    return [slot[e : e + 1, :] == wanted for e in range(experts)]


def stream_kernel(
    query_ref,
    local_ref,
    gate_gain_ref,
    residual_ref,
    carried_ref,
    since_ref,
    expert_gain_ref,
    selector_ref,
    stream_ref,
    *rest,
):
    *bin_refs, attention_ref = rest
    tokens, width = query_ref.shape
    heads = width // HEAD
    since = since_ref[...]
    total = jnp.zeros((tokens, HEAD), F32)
    for h in range(heads):
        carried_out = jnp.dot(
            query_ref[:, lane_block(h)], carried_ref[h], preferred_element_type=F32
        )
        attention = local_ref[:, lane_block(h)] + since[:, h : h + 1] * carried_out
        attention_ref[:, lane_block(h)] = attention
        total = total + attention * attention
    inverse = lax.rsqrt(jnp.sum(total, axis=1, keepdims=True) / width + 1e-05)
    total = jnp.zeros((tokens, HEAD), F32)
    for h in range(heads):
        gated = attention_ref[:, lane_block(h)] * inverse * gate_gain_ref[:, lane_block(h)]
        stream = (residual_ref[:, lane_block(h)].astype(F32) + gated).astype(BF16)
        stream_ref[:, lane_block(h)] = stream
        wide = stream.astype(F32)
        total = total + wide * wide
    inverse = lax.rsqrt(jnp.sum(total, axis=1, keepdims=True) / width + 1e-05)
    experts, rows, _ = bin_refs[0].shape
    count = experts * rows
    size = 2 * HEAD
    for start in range(0, width, size):
        columns = slice(start, start + size)
        wide = stream_ref[:, columns].astype(F32)
        entry = (wide * inverse * expert_gain_ref[:, columns]).astype(BF16)
        picked = jnp.dot(selector_ref[...], entry, preferred_element_type=F32).astype(BF16)
        for c, bin_ref in enumerate(bin_refs):
            part = picked[c * count : (c + 1) * count]
            bin_ref[:, :, columns] = part.reshape(experts, rows, size)


def first_mix_kernel(
    stream_ref, index_ref, router_ref, returned_ref, total_ref, later_high_ref, later_low_ref
):
    experts, rows, width = returned_ref.shape
    first, second, slot = places(index_ref, experts)
    scale = jnp.where(first, router_ref[0:1, :], 0.0) + jnp.where(second, router_ref[1:2, :], 0.0)
    weights = []
    for c in range(2):
        masks = chunk_rows(slot, c, rows)
        chosen = jnp.concatenate(
            [jnp.where(m, scale[e : e + 1, :], 0.0) for e, m in enumerate(masks)], axis=0
        ).T
        high = chosen.astype(BF16)
        weights.append((high, (chosen - high.astype(F32)).astype(BF16)))
    later_high_ref[...], later_low_ref[...] = weights[1]
    high, low = weights[0]
    for h in range(width // HEAD // 4):
        columns = slice(h * 4 * HEAD, (h + 1) * 4 * HEAD)
        returned = returned_ref[:, :, columns].reshape(experts * rows, 4 * HEAD)
        total = stream_ref[:, columns].astype(F32)
        total = total + jnp.dot(high, returned, preferred_element_type=F32)
        total_ref[:, columns] = total + jnp.dot(low, returned, preferred_element_type=F32)


def last_mix_kernel(total_ref, high_ref, low_ref, returned_ref, out_ref, mixed_ref, stored):
    experts, rows, width = returned_ref.shape
    groups = stored.shape[0]
    size = width // groups
    copies = []
    for g in range(groups):
        columns = slice(g * size, (g + 1) * size)
        returned = returned_ref[:, :, columns].reshape(experts * rows, size)
        total = total_ref[:, columns]
        total = total + jnp.dot(high_ref[...], returned, preferred_element_type=F32)
        total = total + jnp.dot(low_ref[...], returned, preferred_element_type=F32)
        mixed_ref[:, columns] = total.astype(BF16)
        part = pl.ds(g * size, size)
        copies.append(
            pltpu.make_async_copy(mixed_ref.at[:, part], out_ref.at[:, part], stored.at[g])
        )
        copies[-1].start()
    for copy in copies:
        copy.wait()


def expert_kernel(
    own_ref,
    left_ref,
    right_ref,
    far_ref,
    up_own_ref,
    up_other_ref,
    down_own_ref,
    down_other_ref,
    out_own_ref,
    out_left_ref,
    out_right_ref,
    out_far_ref,
    rows_ref,
    up_ref,
    down_ref,
    turned_ref,
    hidden_ref,
    up_sem,
    down_sem,
):
    count = own_ref.shape[0]
    tiles, _, tile, width = up_ref.shape
    units = down_own_ref.shape[0]
    parts, _, columns = down_ref.shape
    each = tiles // 2

    def up_copies(k):
        source = (up_own_ref, up_other_ref)[k // each]
        part = source.at[:, pl.ds(k % each * tile, tile), :]
        return [pltpu.make_async_copy(part, up_ref.at[k], up_sem.at[k])]

    def down_copies(k):
        return [
            pltpu.make_async_copy(
                source.at[:, pl.ds(k * columns, columns)],
                down_ref.at[k, pl.ds(place * units, units), :],
                down_sem.at[k, place],
            )
            for place, source in enumerate((down_own_ref, down_other_ref))
        ]

    loads = [up_copies(k) for k in range(tiles)] + [down_copies(k) for k in range(parts)]
    in_flight = 2

    def start(k):
        if k < len(loads):
            for copy in loads[k]:
                copy.start()

    def arrive(k):
        for copy in loads[k]:
            copy.wait()
        start(k + in_flight)

    for k in range(in_flight):
        start(k)
    rows_ref[0:count] = own_ref[...]
    rows_ref[count : 2 * count] = left_ref[...]
    rows_ref[2 * count : 3 * count] = right_ref[...]
    rows_ref[3 * count :] = far_ref[...]
    for k in range(tiles):
        arrive(k)
        both = up_ref[k].reshape(2 * tile, width)
        pair = lax.dot_general(both, rows_ref[...], NT, preferred_element_type=F32)
        gate, up = (pair[:tile], pair[tile:])
        hidden = gate / (1.0 + jnp.exp(-gate)) * up
        turned_ref[k * tile : (k + 1) * tile, :] = hidden.astype(BF16)
    hidden_ref[...] = turned_ref[...].T
    for k in range(parts):
        arrive(tiles + k)
        out = jnp.dot(hidden_ref[...], down_ref[k], preferred_element_type=F32).astype(BF16)
        for place, ref in enumerate((out_own_ref, out_left_ref, out_right_ref, out_far_ref)):
            ref[:, k * columns : (k + 1) * columns] = out[place * count : (place + 1) * count]


def expert_rows(blocks, up_own, up_other, down_own, down_other):
    count, width = blocks[0].shape
    units = down_own.shape[0]
    tiles, parts = (4, 4)
    tile, columns = (2 * units // tiles, width // parts)
    in_place = [pl.BlockSpec(memory_space=pltpu.HBM)] * 4
    return pl.pallas_call(
        expert_kernel,
        in_specs=vmem(len(blocks)) + in_place,
        out_specs=vmem(4),
        out_shape=[jax.ShapeDtypeStruct((count, width), BF16)] * 4,
        scratch_shapes=[
            pltpu.VMEM((4 * count, width), BF16),
            pltpu.VMEM((tiles, 2, tile, width), BF16),
            pltpu.VMEM((parts, 2 * units, columns), BF16),
            pltpu.VMEM((2 * units, 4 * count), BF16),
            pltpu.VMEM((4 * count, 2 * units), BF16),
            pltpu.SemaphoreType.DMA((tiles,)),
            pltpu.SemaphoreType.DMA((parts, 2)),
        ],
        cost_estimate=pl.CostEstimate(
            flops=4 * count * 2 * units * width * 6,
            bytes_accessed=6 * units * width * 2 + 8 * count * width * 2,
            transcendentals=0,
        ),
        compiler_params=pltpu.CompilerParams(vmem_limit_bytes=46 * MIB),
    )(*blocks, up_own, up_other, down_own, down_other)


def body(
    queries,
    key_rows,
    value_rows,
    gate_logits,
    residual_in,
    decay_rate,
    attention_gain,
    expert_gain,
    expert_index,
    router_weight,
    gate_up_weight,
    down_weight,
):
    chips, experts = (lax.axis_size("x"), lax.axis_size("seq"))
    tokens, width = queries.shape
    heads = decay_rate.shape[1]
    chunks = 2
    slots = tokens * expert_index.shape[1] // experts
    rows = slots // chunks
    count = experts * rows

    swap = lambda a: lax.ppermute(a, "core", [(0, 1), (1, 0)])
    go_ahead = lambda a: lax.ppermute(a, "x", [(i, (i + 1) % chips) for i in range(chips)])
    go_back = lambda a: lax.ppermute(a, "x", [(i, (i - 1) % chips) for i in range(chips)])
    to_later = lambda a, k: lax.ppermute(a, "x", [(i, (i + k) % chips) for i in range(chips)])
    plane = ("core", "seq")
    after = lambda value, *earlier: lax.optimization_barrier((value, earlier))[0]
    exchange = lambda a, axis: lax.all_to_all(a, axis, split_axis=0, concat_axis=0, tiled=True)
    shape = jax.ShapeDtypeStruct

    up_own = jnp.transpose(gate_up_weight[0], (1, 2, 0))
    down_own = down_weight[0]

    sent, by_head = whole_call(
        state_kernel,
        [
            shape((heads, HEAD + EXTRA, HEAD), BF16),
            shape((heads, tokens), F32),
        ],
        [decay_rate.T, key_rows, value_rows],
        2 * tokens * width * HEAD,
        62,
        [
            pltpu.VMEM((heads, tokens), F32),
            pltpu.VMEM((tokens, width), BF16),
            pltpu.VMEM((tokens, width), BF16),
            pltpu.SemaphoreType.DMA((2, 4)),
            pltpu.SemaphoreType.DMA,
        ],
        (0, 1, 2),
    )
    arrived = exchange(sent, plane)
    index = expert_index.T
    local_out, since, selector, gate_gain = whole_call(
        functools.partial(local_kernel, experts, chunks),
        [
            shape((tokens, width), F32),
            shape((tokens, heads), F32),
            shape((chunks * count, tokens), BF16),
            shape((tokens, width), F32),
        ],
        [
            queries,
            key_rows,
            value_rows,
            by_head,
            index,
            gate_logits,
            attention_gain[None, :],
        ],
        4 * tokens * width * tokens,
        16,
    )
    within, kept, total = whole_call(
        scan_kernel,
        [
            shape((heads, HEAD, HEAD), F32),
            shape((heads, EXTRA, HEAD), F32),
            shape((HEAD + EXTRA, HEAD), BF16),
        ],
        [after(arrived, local_out)],
        2 * heads * HEAD * HEAD,
        8,
    )
    distance = lax.broadcasted_iota(jnp.int32, (chips - 1, HEAD), 0) + 1
    earlier = (distance <= lax.axis_index("x")).astype(F32)
    totals = [to_later(total, k) for k in range(1, chips)]
    (carried,) = whole_call(
        carry_kernel,
        [shape((heads, HEAD, HEAD), BF16)],
        [within, kept, earlier, *totals],
        2 * heads * HEAD * HEAD,
        8,
    )
    carried_low = exchange(carried, plane)
    stream, *bins = whole_call(
        stream_kernel,
        [shape((tokens, width), BF16)] + [shape((experts, rows, width), BF16)] * chunks,
        [
            queries,
            local_out,
            gate_gain,
            residual_in,
            carried_low,
            since,
            expert_gain[None, :],
            selector,
        ],
        2 * tokens * width * (HEAD + chunks * count),
        8,
        [pltpu.VMEM((tokens, width), F32)],
    )

    up_other = swap(after(up_own, stream))
    down_other = swap(after(down_own, stream))
    weights = (up_own, up_other, down_own, down_other)
    wide = lambda a: a.astype(F32)
    plus = lambda *terms: functools.reduce(jnp.add, map(wide, terms)).astype(BF16)

    own_a, own_b = (exchange(bin_rows, "seq").reshape(count, width) for bin_rows in bins)
    left_a, right_a = (go_ahead(own_a), go_back(own_a))
    far_a = go_ahead(after(left_a, own_b))
    right_b = go_back(after(own_b, right_a, down_other))
    left_b = go_ahead(after(own_b, far_a))
    far_b = go_back(right_b)
    out_own_a, out_left_a, out_right_a, out_far_a = expert_rows(
        (own_a, left_a, right_a, far_a), *weights
    )
    pass_a, back_a = (go_ahead(out_far_a), go_back(out_left_a))
    out_own_b, out_left_b, out_right_b, out_far_b = expert_rows(
        (own_b, left_b, right_b, far_b), *weights
    )
    pass_b = go_back(after(out_far_b, pass_a, back_a))
    ahead_a = go_ahead(plus(out_right_a, pass_a))
    ahead_b = go_ahead(after(out_right_b, ahead_a))
    to_left_b = plus(out_left_b, pass_b)
    back_b = go_back(to_left_b)
    home = lambda *terms: plus(*terms).reshape(experts, rows, width)
    returned_a = exchange(after(home(out_own_a, ahead_a, back_a), to_left_b), "seq")
    total, high, low = whole_call(
        first_mix_kernel,
        [shape((tokens, width), F32)] + [shape((tokens, count), BF16)] * 2,
        [stream, index, router_weight.T, returned_a],
        4 * tokens * width * count,
        8,
    )
    returned_b = exchange(home(after(out_own_b, total), ahead_b, back_b), "seq")
    (out,) = whole_call(
        last_mix_kernel,
        [shape((tokens, width), BF16)],
        [total, high, low, returned_b],
        4 * tokens * width * count,
        8,
        [pltpu.VMEM((tokens, width), BF16), pltpu.SemaphoreType.DMA((4,))],
        out_in_place=(0,),
    )
    return out


def solution(mesh):
    groups, experts = (mesh.shape["grp"], mesh.shape["seq"])
    split = Mesh(mesh.devices.reshape(groups // 2, 2, experts), ("x", "core", "seq"))
    rows = P(("x", "core", "seq"), None)
    return jax.shard_map(
        body,
        mesh=split,
        in_specs=(
            rows,
            rows,
            rows,
            rows,
            rows,
            rows,
            P(),
            P(),
            rows,
            rows,
            P("seq", None, None, ("x", "core")),
            P("seq", ("x", "core"), None),
        ),
        out_specs=rows,
        check_vma=False,
    )
```

```python
import functools

import jax
import jax.numpy as jnp
from jax import lax
from jax.experimental import pallas as pl
from jax.experimental.pallas import tpu as pltpu
from jax.sharding import Mesh
from jax.sharding import PartitionSpec as P

F32, BF16 = (jnp.float32, jnp.bfloat16)
HEAD = 128
EXTRA = 8
MIB = 1 << 20
NT = (((1,), (1,)), ((), ()))
TN = (((0,), (0,)), ((), ()))


def vmem(count):
    return [pl.BlockSpec(memory_space=pltpu.VMEM)] * count


def whole_call(kernel, outs, args, flops, limit, scratch=(), in_place=(), out_in_place=()):
    moved = sum(a.size * a.dtype.itemsize for a in (*args, *outs))
    return pl.pallas_call(
        kernel,
        out_shape=outs,
        in_specs=[
            pl.BlockSpec(memory_space=pltpu.HBM if place in in_place else pltpu.VMEM)
            for place in range(len(args))
        ],
        out_specs=[
            pl.BlockSpec(memory_space=pltpu.HBM if place in out_in_place else pltpu.VMEM)
            for place in range(len(outs))
        ],
        scratch_shapes=list(scratch),
        cost_estimate=pl.CostEstimate(flops=flops, bytes_accessed=moved, transcendentals=0),
        compiler_params=pltpu.CompilerParams(vmem_limit_bytes=limit * MIB),
    )(*args)


def lane_block(h):
    return slice(h * HEAD, (h + 1) * HEAD)


def state_kernel(
    rates_in_ref,
    key_rows_ref,
    value_rows_ref,
    sent_ref,
    by_head_ref,
    rates_ref,
    key_ref,
    value_ref,
    loaded,
    rates_loaded,
):
    heads, tokens = rates_ref.shape
    rates_copy = pltpu.make_async_copy(rates_in_ref, rates_ref, rates_loaded)
    rates_copy.start()
    groups = loaded.shape[1]
    columns = heads * HEAD // groups
    copies = [
        [
            pltpu.make_async_copy(
                source.at[:, pl.ds(g * columns, columns)],
                target.at[:, pl.ds(g * columns, columns)],
                loaded.at[place, g],
            )
            for place, (source, target) in enumerate(
                ((key_rows_ref, key_ref), (value_rows_ref, value_ref))
            )
        ]
        for g in range(groups)
    ]
    for pair in copies:
        for copy in pair:
            copy.start()
    rates_copy.wait()
    at = lambda dim: lax.broadcasted_iota(jnp.int32, (tokens, tokens), dim)
    upto = (at(0) <= at(1)).astype(F32)
    by_head = jnp.dot(
        rates_ref[...], upto, precision=lax.Precision.HIGHEST, preferred_element_type=F32
    )
    by_head_ref[...] = by_head
    fade = jnp.exp(by_head - by_head[:, tokens - 1 :])
    keep = jnp.broadcast_to(jnp.exp(-by_head[:, tokens - 1 :]), (heads, HEAD))
    high = keep.astype(BF16).astype(F32)
    middle = (keep - high).astype(BF16).astype(F32)
    low = keep - high - middle
    row = lax.broadcasted_iota(jnp.int32, (EXTRA, HEAD), 0)
    for h in range(heads):
        if h % (heads // groups) == 0:
            for copy in copies[h // (heads // groups)]:
                copy.wait()
        turned = key_ref[:, lane_block(h)].T
        faded = (turned.astype(F32) * fade[h : h + 1, :]).astype(BF16)
        state = jnp.dot(faded, value_ref[:, lane_block(h)], preferred_element_type=F32)
        tail = jnp.where(row == 0, high[h : h + 1], 0.0)
        tail = jnp.where(row == 1, middle[h : h + 1], tail)
        tail = jnp.where(row == 2, low[h : h + 1], tail).astype(BF16)
        sent_ref[h, :HEAD, :] = state.astype(BF16)
        sent_ref[h, HEAD:, :] = tail


def scan_kernel(arrived_ref, within_ref, kept_ref, total_ref):
    def step(block, carry):
        state, kept = carry
        within_ref[block] = state
        kept_ref[block] = kept
        tail = arrived_ref[block, HEAD:, :].astype(F32)
        keep = tail[0:1] + tail[1:2] + tail[2:3]
        return keep * state + arrived_ref[block, :HEAD, :].astype(F32), keep * kept

    start = (jnp.zeros((HEAD, HEAD), F32), jnp.ones((EXTRA, HEAD), F32))
    state, kept = lax.fori_loop(0, within_ref.shape[0], step, start, unroll=4)
    total_ref[:HEAD, :] = state.astype(BF16)
    high = kept.astype(BF16).astype(F32)
    middle = (kept - high).astype(BF16).astype(F32)
    row = lax.broadcasted_iota(jnp.int32, kept.shape, 0)
    tail = jnp.where(row == 0, high, jnp.where(row == 1, middle, kept - high - middle))
    total_ref[HEAD:, :] = tail.astype(BF16)


def carry_kernel(within_ref, kept_ref, earlier_ref, *rest):
    *total_refs, carried_ref = rest
    before = jnp.zeros((HEAD, HEAD), F32)
    for place, total_ref in reversed(list(enumerate(total_refs))):
        tail = total_ref[HEAD:, :].astype(F32)
        keep = tail[0:1] + tail[1:2] + tail[2:3]
        longer = total_ref[:HEAD, :].astype(F32) + keep * before
        before = jnp.where(earlier_ref[place : place + 1, :] > 0.0, longer, before)

    def step(block, _):
        carried = within_ref[block] + kept_ref[block, 0:1, :] * before
        carried_ref[block] = carried.astype(BF16)
        return 0

    lax.fori_loop(0, carried_ref.shape[0], step, 0, unroll=4)


def local_kernel(
    experts,
    chunks,
    query_ref,
    key_ref,
    value_ref,
    by_head_ref,
    index_ref,
    gate_ref,
    attention_gain_ref,
    out_ref,
    since_ref,
    selector_ref,
    gate_gain_ref,
):
    heads, tokens = by_head_ref.shape
    by_token = by_head_ref[...].T
    since_ref[...] = jnp.exp(-by_token)
    slot = places(index_ref, experts)[2]
    count = selector_ref.shape[0] // chunks
    for c in range(chunks):
        masks = chunk_rows(slot, c, count // experts)
        selector = jnp.concatenate([m.astype(F32) for m in masks], axis=0)
        selector_ref[c * count : (c + 1) * count, :] = selector.astype(BF16)
    at = lambda dim: lax.broadcasted_iota(jnp.int32, (tokens, tokens), dim)
    causal = at(0) >= at(1)
    for h in range(heads):
        scores = lax.dot_general(
            query_ref[:, lane_block(h)], key_ref[:, lane_block(h)], NT, preferred_element_type=F32
        )
        spacing = by_head_ref[h : h + 1, :] - by_token[:, h : h + 1]
        fading = jnp.exp(jnp.minimum(spacing, 0.0))
        weights = jnp.where(causal, scores * fading, 0.0).astype(BF16)
        out_ref[:, lane_block(h)] = jnp.dot(
            weights, value_ref[:, lane_block(h)], preferred_element_type=F32
        )
        gate = gate_ref[:, lane_block(h)].astype(F32)
        gain = attention_gain_ref[:, lane_block(h)]
        gate_gain_ref[:, lane_block(h)] = gain / (1.0 + jnp.exp(-gate))


def places(index_ref, experts):
    tokens = index_ref.shape[1]
    expert = lax.broadcasted_iota(jnp.int32, (experts, tokens), 0)
    first, second = (index_ref[0:1, :] == expert, index_ref[1:2, :] == expert)
    named = (first | second).astype(F32)
    at = lambda dim: lax.broadcasted_iota(jnp.int32, (tokens, tokens), dim)
    earlier = (at(0) < at(1)).astype(BF16)
    slot = jnp.dot(named.astype(BF16), earlier, preferred_element_type=F32)
    return first, second, jnp.where(named > 0.0, slot, -1.0)


def chunk_rows(slot, chunk, rows):
    experts, tokens = slot.shape
    wanted = lax.broadcasted_iota(jnp.int32, (rows, tokens), 0).astype(F32) + float(chunk * rows)
    return [slot[e : e + 1, :] == wanted for e in range(experts)]


def stream_kernel(
    query_ref,
    local_ref,
    gate_gain_ref,
    residual_ref,
    carried_ref,
    since_ref,
    expert_gain_ref,
    selector_ref,
    stream_ref,
    *rest,
):
    *bin_refs, attention_ref = rest
    tokens, width = query_ref.shape
    heads = width // HEAD
    since = since_ref[...]
    total = jnp.zeros((tokens, HEAD), F32)
    for h in range(heads):
        carried_out = jnp.dot(
            query_ref[:, lane_block(h)], carried_ref[h], preferred_element_type=F32
        )
        attention = local_ref[:, lane_block(h)] + since[:, h : h + 1] * carried_out
        attention_ref[:, lane_block(h)] = attention
        total = total + attention * attention
    inverse = lax.rsqrt(jnp.sum(total, axis=1, keepdims=True) / width + 1e-05)
    total = jnp.zeros((tokens, HEAD), F32)
    for h in range(heads):
        gated = attention_ref[:, lane_block(h)] * inverse * gate_gain_ref[:, lane_block(h)]
        stream = (residual_ref[:, lane_block(h)].astype(F32) + gated).astype(BF16)
        stream_ref[:, lane_block(h)] = stream
        wide = stream.astype(F32)
        total = total + wide * wide
    inverse = lax.rsqrt(jnp.sum(total, axis=1, keepdims=True) / width + 1e-05)
    experts, rows, _ = bin_refs[0].shape
    count = experts * rows
    size = 2 * HEAD
    for start in range(0, width, size):
        columns = slice(start, start + size)
        wide = stream_ref[:, columns].astype(F32)
        entry = (wide * inverse * expert_gain_ref[:, columns]).astype(BF16)
        picked = jnp.dot(selector_ref[...], entry, preferred_element_type=F32).astype(BF16)
        for c, bin_ref in enumerate(bin_refs):
            part = picked[c * count : (c + 1) * count]
            bin_ref[:, :, columns] = part.reshape(experts, rows, size)


def first_mix_kernel(
    stream_ref, index_ref, router_ref, returned_ref, total_ref, later_high_ref, later_low_ref
):
    experts, rows, width = returned_ref.shape
    first, second, slot = places(index_ref, experts)
    scale = jnp.where(first, router_ref[0:1, :], 0.0) + jnp.where(second, router_ref[1:2, :], 0.0)
    weights = []
    for c in range(2):
        masks = chunk_rows(slot, c, rows)
        chosen = jnp.concatenate(
            [jnp.where(m, scale[e : e + 1, :], 0.0) for e, m in enumerate(masks)], axis=0
        ).T
        high = chosen.astype(BF16)
        weights.append((high, (chosen - high.astype(F32)).astype(BF16)))
    later_high_ref[...], later_low_ref[...] = weights[1]
    high, low = weights[0]
    for h in range(width // HEAD // 4):
        columns = slice(h * 4 * HEAD, (h + 1) * 4 * HEAD)
        returned = returned_ref[:, :, columns].reshape(experts * rows, 4 * HEAD)
        total = stream_ref[:, columns].astype(F32)
        total = total + jnp.dot(high, returned, preferred_element_type=F32)
        total_ref[:, columns] = total + jnp.dot(low, returned, preferred_element_type=F32)


def last_mix_kernel(total_ref, high_ref, low_ref, returned_ref, out_ref, mixed_ref, stored):
    experts, rows, width = returned_ref.shape
    groups = stored.shape[0]
    size = width // groups
    copies = []
    for g in range(groups):
        columns = slice(g * size, (g + 1) * size)
        returned = returned_ref[:, :, columns].reshape(experts * rows, size)
        total = total_ref[:, columns]
        total = total + jnp.dot(high_ref[...], returned, preferred_element_type=F32)
        total = total + jnp.dot(low_ref[...], returned, preferred_element_type=F32)
        mixed_ref[:, columns] = total.astype(BF16)
        part = pl.ds(g * size, size)
        copies.append(
            pltpu.make_async_copy(mixed_ref.at[:, part], out_ref.at[:, part], stored.at[g])
        )
        copies[-1].start()
    for copy in copies:
        copy.wait()


def expert_kernel(
    own_ref,
    left_ref,
    right_ref,
    far_ref,
    up_own_ref,
    up_other_ref,
    down_own_ref,
    down_other_ref,
    out_own_ref,
    out_left_ref,
    out_right_ref,
    out_far_ref,
    rows_ref,
    up_ref,
    down_ref,
    turned_ref,
    hidden_ref,
    up_sem,
    down_sem,
):
    count = own_ref.shape[0]
    tiles, _, tile, width = up_ref.shape
    units = down_own_ref.shape[0]
    parts, _, columns = down_ref.shape
    each = tiles // 2

    def up_copies(k):
        source = (up_own_ref, up_other_ref)[k // each]
        part = source.at[:, pl.ds(k % each * tile, tile), :]
        return [pltpu.make_async_copy(part, up_ref.at[k], up_sem.at[k])]

    def down_copies(k):
        return [
            pltpu.make_async_copy(
                source.at[:, pl.ds(k * columns, columns)],
                down_ref.at[k, pl.ds(place * units, units), :],
                down_sem.at[k, place],
            )
            for place, source in enumerate((down_own_ref, down_other_ref))
        ]

    loads = [up_copies(k) for k in range(tiles)] + [down_copies(k) for k in range(parts)]
    in_flight = 2

    def start(k):
        if k < len(loads):
            for copy in loads[k]:
                copy.start()

    def arrive(k):
        for copy in loads[k]:
            copy.wait()
        start(k + in_flight)

    for k in range(in_flight):
        start(k)
    rows_ref[0:count] = own_ref[...]
    rows_ref[count : 2 * count] = left_ref[...]
    rows_ref[2 * count : 3 * count] = right_ref[...]
    rows_ref[3 * count :] = far_ref[...]
    for k in range(tiles):
        arrive(k)
        both = up_ref[k].reshape(2 * tile, width)
        pair = lax.dot_general(both, rows_ref[...], NT, preferred_element_type=F32)
        gate, up = (pair[:tile], pair[tile:])
        hidden = gate / (1.0 + jnp.exp(-gate)) * up
        turned_ref[k * tile : (k + 1) * tile, :] = hidden.astype(BF16)
    hidden_ref[...] = turned_ref[...].T
    for k in range(parts):
        arrive(tiles + k)
        out = jnp.dot(hidden_ref[...], down_ref[k], preferred_element_type=F32).astype(BF16)
        for place, ref in enumerate((out_own_ref, out_left_ref, out_right_ref, out_far_ref)):
            ref[:, k * columns : (k + 1) * columns] = out[place * count : (place + 1) * count]


def expert_rows(blocks, up_own, up_other, down_own, down_other):
    count, width = blocks[0].shape
    units = down_own.shape[0]
    tiles, parts = (4, 4)
    tile, columns = (2 * units // tiles, width // parts)
    in_place = [pl.BlockSpec(memory_space=pltpu.HBM)] * 4
    return pl.pallas_call(
        expert_kernel,
        in_specs=vmem(len(blocks)) + in_place,
        out_specs=vmem(4),
        out_shape=[jax.ShapeDtypeStruct((count, width), BF16)] * 4,
        scratch_shapes=[
            pltpu.VMEM((4 * count, width), BF16),
            pltpu.VMEM((tiles, 2, tile, width), BF16),
            pltpu.VMEM((parts, 2 * units, columns), BF16),
            pltpu.VMEM((2 * units, 4 * count), BF16),
            pltpu.VMEM((4 * count, 2 * units), BF16),
            pltpu.SemaphoreType.DMA((tiles,)),
            pltpu.SemaphoreType.DMA((parts, 2)),
        ],
        cost_estimate=pl.CostEstimate(
            flops=4 * count * 2 * units * width * 6,
            bytes_accessed=6 * units * width * 2 + 8 * count * width * 2,
            transcendentals=0,
        ),
        compiler_params=pltpu.CompilerParams(vmem_limit_bytes=46 * MIB),
    )(*blocks, up_own, up_other, down_own, down_other)


def body(
    queries,
    key_rows,
    value_rows,
    gate_logits,
    residual_in,
    decay_rate,
    attention_gain,
    expert_gain,
    expert_index,
    router_weight,
    gate_up_weight,
    down_weight,
):
    chips, experts = (lax.axis_size("x"), lax.axis_size("seq"))
    tokens, width = queries.shape
    heads = decay_rate.shape[1]
    chunks = 2
    slots = tokens * expert_index.shape[1] // experts
    rows = slots // chunks
    count = experts * rows

    swap = lambda a: lax.ppermute(a, "core", [(0, 1), (1, 0)])
    go_ahead = lambda a: lax.ppermute(a, "x", [(i, (i + 1) % chips) for i in range(chips)])
    go_back = lambda a: lax.ppermute(a, "x", [(i, (i - 1) % chips) for i in range(chips)])
    to_later = lambda a, k: lax.ppermute(a, "x", [(i, (i + k) % chips) for i in range(chips)])
    plane = ("core", "seq")
    after = lambda value, *earlier: lax.optimization_barrier((value, earlier))[0]
    exchange = lambda a, axis: lax.all_to_all(a, axis, split_axis=0, concat_axis=0, tiled=True)
    shape = jax.ShapeDtypeStruct

    up_own = jnp.transpose(gate_up_weight[0], (1, 2, 0))
    down_own = down_weight[0]

    sent, by_head = whole_call(
        state_kernel,
        [
            shape((heads, HEAD + EXTRA, HEAD), BF16),
            shape((heads, tokens), F32),
        ],
        [decay_rate.T, key_rows, value_rows],
        2 * tokens * width * HEAD,
        62,
        [
            pltpu.VMEM((heads, tokens), F32),
            pltpu.VMEM((tokens, width), BF16),
            pltpu.VMEM((tokens, width), BF16),
            pltpu.SemaphoreType.DMA((2, 2)),
            pltpu.SemaphoreType.DMA,
        ],
        (0, 1, 2),
    )
    arrived = exchange(sent, plane)
    index = expert_index.T
    local_out, since, selector, gate_gain = whole_call(
        functools.partial(local_kernel, experts, chunks),
        [
            shape((tokens, width), F32),
            shape((tokens, heads), F32),
            shape((chunks * count, tokens), BF16),
            shape((tokens, width), F32),
        ],
        [
            queries,
            key_rows,
            value_rows,
            by_head,
            index,
            gate_logits,
            attention_gain[None, :],
        ],
        4 * tokens * width * tokens,
        16,
    )
    within, kept, total = whole_call(
        scan_kernel,
        [
            shape((heads, HEAD, HEAD), F32),
            shape((heads, EXTRA, HEAD), F32),
            shape((HEAD + EXTRA, HEAD), BF16),
        ],
        [after(arrived, local_out)],
        2 * heads * HEAD * HEAD,
        8,
    )
    distance = lax.broadcasted_iota(jnp.int32, (chips - 1, HEAD), 0) + 1
    earlier = (distance <= lax.axis_index("x")).astype(F32)
    totals = [to_later(total, k) for k in range(1, chips)]
    (carried,) = whole_call(
        carry_kernel,
        [shape((heads, HEAD, HEAD), BF16)],
        [within, kept, earlier, *totals],
        2 * heads * HEAD * HEAD,
        8,
    )
    carried_low = exchange(carried, plane)
    stream, *bins = whole_call(
        stream_kernel,
        [shape((tokens, width), BF16)] + [shape((experts, rows, width), BF16)] * chunks,
        [
            queries,
            local_out,
            gate_gain,
            residual_in,
            carried_low,
            since,
            expert_gain[None, :],
            selector,
        ],
        2 * tokens * width * (HEAD + chunks * count),
        8,
        [pltpu.VMEM((tokens, width), F32)],
    )

    up_other = swap(after(up_own, stream))
    down_other = swap(after(down_own, stream))
    weights = (up_own, up_other, down_own, down_other)
    wide = lambda a: a.astype(F32)
    plus = lambda *terms: functools.reduce(jnp.add, map(wide, terms)).astype(BF16)

    own_a, own_b = (exchange(bin_rows, "seq").reshape(count, width) for bin_rows in bins)
    left_a, right_a = (go_ahead(own_a), go_back(own_a))
    far_a = go_ahead(after(left_a, own_b))
    right_b = go_back(after(own_b, right_a, down_other))
    left_b = go_ahead(after(own_b, far_a))
    far_b = go_back(right_b)
    out_own_a, out_left_a, out_right_a, out_far_a = expert_rows(
        (own_a, left_a, right_a, far_a), *weights
    )
    pass_a, back_a = (go_ahead(out_far_a), go_back(out_left_a))
    out_own_b, out_left_b, out_right_b, out_far_b = expert_rows(
        (own_b, left_b, right_b, far_b), *weights
    )
    pass_b = go_back(after(out_far_b, pass_a, back_a))
    ahead_a = go_ahead(plus(out_right_a, pass_a))
    ahead_b = go_ahead(after(out_right_b, ahead_a))
    to_left_b = plus(out_left_b, pass_b)
    back_b = go_back(to_left_b)
    home = lambda *terms: plus(*terms).reshape(experts, rows, width)
    returned_a = exchange(after(home(out_own_a, ahead_a, back_a), to_left_b), "seq")
    total, high, low = whole_call(
        first_mix_kernel,
        [shape((tokens, width), F32)] + [shape((tokens, count), BF16)] * 2,
        [stream, index, router_weight.T, returned_a],
        4 * tokens * width * count,
        8,
    )
    returned_b = exchange(home(after(out_own_b, total), ahead_b, back_b), "seq")
    (out,) = whole_call(
        last_mix_kernel,
        [shape((tokens, width), BF16)],
        [total, high, low, returned_b],
        4 * tokens * width * count,
        8,
        [pltpu.VMEM((tokens, width), BF16), pltpu.SemaphoreType.DMA((4,))],
        out_in_place=(0,),
    )
    return out


def solution(mesh):
    groups, experts = (mesh.shape["grp"], mesh.shape["seq"])
    split = Mesh(mesh.devices.reshape(groups // 2, 2, experts), ("x", "core", "seq"))
    rows = P(("x", "core", "seq"), None)
    return jax.shard_map(
        body,
        mesh=split,
        in_specs=(
            rows,
            rows,
            rows,
            rows,
            rows,
            rows,
            P(),
            P(),
            rows,
            rows,
            P("seq", None, None, ("x", "core")),
            P("seq", ("x", "core"), None),
        ),
        out_specs=rows,
        check_vma=False,
    )
```
